32 devices in a mesh: groups: 2 (over y), sky: 4 (over z), shell: 2 (over x), sub: 2 (over core).
Axes of the slice: x: 2, y: 2, z: 4, core: 2. Of those that a mesh axis runs over, the one named last changes fastest.
Arguments:
- part_cycle: int32 [2, 2048, 256], P('shell', ('sky', 'sub')), may hold values from 0 to 1
- part_pixel: int32 [2, 2048, 256], P('shell', ('sky', 'sub')), may hold values from 0 to 127
- part_mass: float32 [2, 2048, 256], P('shell', ('sky', 'sub')), may hold values from 0.3 to 3
- tile_block: int32 [2, 2048, 1], P('shell', ('sky', 'sub')), may hold values from 0 to 7; in each aligned block of 256 rows (0 to 255, 256 to 511, ..., all dimensions but the last counted through in order) at most 128 rows name the same one
- tile_shell: int32 [2, 2048], P('shell', ('sky', 'sub')), may hold values from 0 to 1
- tile_pixel: int32 [2, 2048], P('shell', ('sky', 'sub')), may hold values from 0 to 63
- harmonic_basis: bfloat16 [128, 16, 4096], P('sky', 'sub'), may hold values from -1.5 to 1.5
- lens_weight: float32 [4, 4], replicated, may hold values from 0.2 to 1
Outputs:
- convergence: float32 [8, 128, 2, 4096], P(('groups', 'shell'), 'sky', None, 'sub'), parts along dimension 0
The draws below stay inside these ranges and needn't reach their ends.
There are 2 independent parts, one for each index of `groups`. The reference program is written for one: setup_inputs(seed, part) draws one part's arguments, and reference() takes and returns one part's arrays. A program takes and returns all parts, laid end to end along the dimension named above; an argument that names none is the same for every part. Nothing has to cross between parts.
Inputs may be any that keep to these rules, and one draw needn't show every extreme that they name: `tile_block`: among the rows of one device no cycle block is named by more than 128 tiles, and in some device one block is named by exactly 128.
All inputs are finite; a program needn't handle non-finite values.
Results may differ from the reference program's by a relative error of at most 0.0015.
Values may be sent and summed in bfloat16 or wider, within the bound.
A program may use at most 192 MiB of HBM per device.

```python
import math
import jax
import jax.numpy as jnp
import numpy as np
from jax import lax

NP = 8192
M = 128
L = 4096
TP = 128
CYCLE_DEV = 2
SHELL_DEV = 2
TILES_DEV = 256
PART_TILE = 256
BLOCKS = 8
CYCLES = 16
NBLK = 64
CAP = 128
TILES_ROW = 2048
SHELLS = 4
SOURCES = 4
N_SHELL = 2


def touch_ends(drawn, rng, least, top_value):
    dims = drawn.shape
    index_at = [jax.random.randint(jax.random.fold_in(rng, axis), (), 0, dims[axis]) for axis in range(len(dims))]
    drawn = drawn.at[tuple(index_at)].set(least)
    longest = dims.index(max(dims))
    index_at[longest] = (index_at[longest] + 1) % dims[longest]
    return drawn.at[tuple(index_at)].set(top_value)


def level_of(own_key, dims, cuts, least, largest):
    def one(position, blocks):
        heights = jax.random.uniform(jax.random.fold_in(jax.random.fold_in(own_key, 6), position), (blocks,), jnp.float32, least / len(cuts), largest / len(cuts))
        return jnp.repeat(jnp.exp(heights), dims[position] // blocks).reshape((-1,) + (1,) * (len(dims) - position - 1))

    loudness = one(*cuts[0])
    for cut in cuts[1:]:
        loudness = loudness * one(*cut)
    return loudness


def deal_out(own_key, own, number, rows, number_of, top, most, skew):
    order = jax.random.permutation(own_key, number_of)
    heavy_load, common = shares(number_of, rows * top, most, skew, True), shares(number_of, rows * top, most, skew, False)
    places = jnp.arange(number_of)

    def named(tallies, turn):
        used = int((tallies > 0).sum())
        fixed = max(1, used // 4)
        passed = fixed + (places - fixed + turn * (used - fixed)) % max(1, number_of - fixed)
        return jnp.zeros((number_of,), jnp.int32).at[order[jnp.where(places < fixed, places, passed)]].set(jnp.asarray(tallies, jnp.int32))

    tallies = jnp.where(number % 4 == 0, named(heavy_load, number // 4), named(common, number - number // 4 - 1))
    mixed = jax.random.permutation(jax.random.fold_in(own, 3), number_of)
    source_of, sink = mixed[0:number_of // 2 * 2:2], mixed[1:number_of // 2 * 2:2]
    slack = jnp.minimum(tallies[source_of] - 1, most - tallies[sink]) // 2
    slack = jnp.where((source_of == order[0]) | (sink == order[0]) | (tallies[sink] == 0), 0, jnp.maximum(slack, 0))
    passed = jax.random.randint(jax.random.fold_in(own, 4), (number_of // 2,), 0, 1 << 20) % (slack + 1)
    tallies = tallies.at[source_of].add(-passed).at[sink].add(passed)
    members = jnp.searchsorted(jnp.cumsum(tallies), jnp.arange(rows * top), side="right").astype(jnp.int32)
    listing = members.reshape(top, rows).T
    listing = listing[jax.random.permutation(jax.random.fold_in(own, 1), rows)]
    turn = jax.random.randint(jax.random.fold_in(own, 2), (rows, 1), 0, top)
    return jnp.take_along_axis(listing, (jnp.arange(top)[None, :] + turn) % top, axis=1)


def shares(amount, total, bound, lean, full):
    weights = [(1 << 20) // math.isqrt(standing ** lean) + 1 for standing in range(1, amount + 1)]
    largest = bound if full else min(bound, max(-(-total // amount), total * weights[0] // sum(weights)))
    least = 1 if total - largest >= amount - 1 else 0
    given, rest = [largest] + [least] * (amount - 1), total - largest - least * (amount - 1)
    while rest > 0:
        candidates = [i for i in range(1, amount) if given[i] < largest] or [i for i in range(1, amount) if given[i] < bound]
        mass, left = sum([weights[i] for i in candidates]), rest
        for i in candidates:
            extra = min(bound - given[i], max(1, left * weights[i] // mass), rest)
            given[i] = given[i] + extra
            rest = rest - extra
    return np.array(given)


def bell_draw(key, dims, scale, bound, cuts=(), kind=jnp.bfloat16):
    factor_of = level_of(key, dims, cuts, -0.22, 0.18) if cuts else 1.0
    result = jax.random.normal(key, dims, jnp.float32) * scale * factor_of
    return jnp.minimum(jnp.maximum(result, -bound), bound).astype(kind)


def setup_inputs(seed: int = 0, part: int = 0) -> dict:
    seeds = jax.random.split(jax.random.key(seed), 9)
    part_cycle = touch_ends(jax.random.randint(seeds[0], (N_SHELL, TILES_ROW, PART_TILE), 0, CYCLE_DEV), jax.random.fold_in(seeds[0], 1), 0, CYCLE_DEV - 1).astype(jnp.int32)
    part_pixel = touch_ends(jax.random.randint(seeds[1], (N_SHELL, TILES_ROW, PART_TILE), 0, TP), jax.random.fold_in(seeds[1], 1), 0, TP - 1).astype(jnp.int32)
    part_mass = jnp.clip(jnp.exp(math.log(3.0) - 2.3025851 * jax.random.uniform(seeds[2], (N_SHELL, TILES_ROW, PART_TILE), jnp.float32) ** level_of(seeds[2], (N_SHELL, TILES_ROW, PART_TILE), ((0, 2), (1, 8)), -0.2, 0.2)), 0.3, 3.0)
    tile_block_keys = jax.random.split(jax.random.fold_in(seeds[3], 1), N_SHELL * TILES_ROW // TILES_DEV)
    tile_block_turns = jax.random.permutation(jax.random.fold_in(seeds[3], 3), N_SHELL * TILES_ROW // TILES_DEV)
    tile_block = jax.vmap(lambda own, number: deal_out(jax.random.fold_in(seeds[3], 2), own, number, TILES_DEV, BLOCKS, 1, CAP, 2))(tile_block_keys, tile_block_turns).reshape((N_SHELL, TILES_ROW, 1))
    tile_shell = touch_ends(jax.random.randint(seeds[4], (N_SHELL, TILES_ROW), 0, SHELL_DEV), jax.random.fold_in(seeds[4], 1), 0, SHELL_DEV - 1).astype(jnp.int32)
    tile_pixel = touch_ends(jax.random.randint(seeds[5], (N_SHELL, TILES_ROW), 0, NBLK), jax.random.fold_in(seeds[5], 1), 0, NBLK - 1).astype(jnp.int32)
    harmonic_basis = bell_draw(seeds[6], (M, CYCLES, L), CYCLES ** -0.5, 1.5, ((0, 4), (1, 2)))
    lens_weight = jnp.clip(jnp.exp(jax.random.uniform(seeds[7], (SOURCES, SHELLS), jnp.float32, math.log(0.2), math.log(1.0))), 0.2, 1.0)
    return dict(part_cycle=part_cycle, part_pixel=part_pixel, part_mass=part_mass, tile_block=tile_block, tile_shell=tile_shell, tile_pixel=tile_pixel, harmonic_basis=harmonic_basis, lens_weight=lens_weight)


precise = lax.Precision.HIGHEST


def deposit(cycle_index, pixel_index, masses):
    cycle_axis = jnp.arange(CYCLE_DEV, dtype=jnp.float32)
    pixel_axis = jnp.arange(TP, dtype=jnp.float32)
    cycle_part = jnp.exp(-0.5 * (cycle_axis[None, None, :] - cycle_index.astype(jnp.float32)[:, :, None]) ** 2)
    pixel_part = jnp.exp(-(pixel_axis[None, None, :] - pixel_index.astype(jnp.float32)[:, :, None]) ** 2 / 18.0)
    weighted = pixel_part * masses[:, :, None]
    return jnp.einsum("tpk,tpj->tkj", cycle_part, weighted, precision=precise)


def fourier_table():
    pixels = jnp.arange(NP, dtype=jnp.int32)
    orders = jnp.arange(M, dtype=jnp.int32)
    phases = (pixels[:, None] * orders[None, :]) % NP
    angles = phases.astype(jnp.float32) * (2.0 * math.pi / NP)
    return jnp.concatenate([jnp.cos(angles), -jnp.sin(angles)], axis=1)


def deposit_block(packed):
    return deposit(packed[0], packed[1], packed[2])


def reference(part_cycle, part_pixel, part_mass, tile_block, tile_shell, tile_pixel, harmonic_basis, lens_weight):
    row_tiles = part_cycle.shape[1]
    tile_count = part_cycle.shape[0] * row_tiles
    cycle_flat = part_cycle.reshape(tile_count // TILES_DEV, TILES_DEV, PART_TILE)
    pixel_flat = part_pixel.reshape(tile_count // TILES_DEV, TILES_DEV, PART_TILE)
    mass_flat = part_mass.reshape(tile_count // TILES_DEV, TILES_DEV, PART_TILE)
    tile_sums = lax.map(deposit_block, (cycle_flat, pixel_flat, mass_flat)).reshape(tile_count, CYCLE_DEV, TP)
    group_of = jnp.arange(tile_count, dtype=jnp.int32) // row_tiles
    shell_of = (group_of * SHELL_DEV + tile_shell.reshape(tile_count)).astype(jnp.int32)
    block_of = tile_block.reshape(tile_count).astype(jnp.int32)
    pixel_of = tile_pixel.reshape(tile_count).astype(jnp.int32)
    sky_map = jnp.zeros((SHELLS, BLOCKS, CYCLE_DEV, NBLK, TP), jnp.float32)
    sky_map = sky_map.at[shell_of, block_of, :, pixel_of, :].add(tile_sums)
    flat_map = sky_map.reshape(SHELLS * CYCLES, NP)
    cycle_modes = jnp.dot(flat_map, fourier_table(), precision=precise) * (2.0 * math.pi / NP)
    cycle_modes = cycle_modes.astype(jnp.bfloat16).reshape(SHELLS, CYCLES, 2, M)
    harmonics = jnp.einsum("mrl,srcm->smcl", harmonic_basis.astype(jnp.float32), cycle_modes.astype(jnp.float32), precision=precise)
    source_ids = jnp.arange(SHELLS, dtype=jnp.int32)
    weights = lens_weight * (source_ids[None, :] <= source_ids[:, None]).astype(jnp.float32)
    return jnp.einsum("js,smcl->jmcl", weights, harmonics, precision=precise)
```

```python
import functools
import math

import jax
import jax.numpy as jnp
import numpy as np
from jax import lax
from jax.experimental import pallas as pl
from jax.experimental.pallas import tpu as pltpu
from jax.sharding import PartitionSpec as P

NP = 8192
M = 128
TP = 128
CYCLE_DEV = 2
SHELL_DEV = 2
NBLK = NP // TP

precise = lax.Precision.HIGHEST
MESH = pl.DeviceIdType.MESH


def tables():
    pixel = np.arange(TP, dtype=np.float64)
    smooth = np.exp(-((pixel[:, None] - pixel[None, :]) ** 2) / 18.0)
    orders = np.arange(M)
    angle = 2.0 * math.pi * ((np.arange(TP)[:, None] * orders[None, :]) % NP) / NP
    real, imag = smooth @ np.cos(angle), -(smooth @ np.sin(angle))
    straight = np.stack([real, imag], axis=2).reshape(TP, 2 * M).T
    crossed = np.stack([-imag, real], axis=2).reshape(TP, 2 * M).T
    turn = 2.0 * math.pi * ((np.arange(NBLK)[:, None] * TP * orders[None, :]) % NP) / NP
    cosine = np.repeat(np.cos(turn), 2, axis=1).T
    sine = np.repeat(-np.sin(turn), 2, axis=1).T
    spectrum = np.concatenate([straight, crossed], axis=0).astype(np.float32)
    turns = np.concatenate([cosine, sine], axis=0).astype(np.float32)
    return spectrum, turns


def deposit_kernel(
    sky_count, owners, cycle_ref, pixel_ref, mass_ref, block_ref, shell_ref, place_ref, spectrum_ref,
    turns_ref, out_ref, pixel_t, mass0_t, mass1_t, hist_ref,
):
    tiles, particles = pixel_ref.shape
    lanes = 128
    rows = 64
    masses = mass_ref[...]
    first = cycle_ref[...] == 0
    for held, value in (
        (pixel_t, pixel_ref[...]),
        (mass0_t, jnp.where(first, masses, 0.0)),
        (mass1_t, jnp.where(first, 0.0, masses)),
    ):
        turned = value.T
        for side in range(tiles // lanes):
            held[side] = turned[:, side * lanes : (side + 1) * lanes]
    for side in range(tiles // lanes):
        columns = slice(side * lanes, (side + 1) * lanes)
        for top in range(0, TP, rows):
            ids = lax.broadcasted_iota(jnp.int32, (rows, lanes), 0) + top

            def step(p, sums):
                here = jnp.broadcast_to(pixel_t[side, pl.ds(p, 1), :], (rows, lanes)) == ids
                one = jnp.broadcast_to(mass0_t[side, pl.ds(p, 1), :], (rows, lanes))
                two = jnp.broadcast_to(mass1_t[side, pl.ds(p, 1), :], (rows, lanes))
                return sums[0] + jnp.where(here, one, 0.0), sums[1] + jnp.where(here, two, 0.0)

            zero = jnp.zeros((rows, lanes), jnp.float32)
            one, two = lax.fori_loop(0, particles, step, (zero, zero), unroll=8)
            hist_ref[0, top : top + rows, columns] = one
            hist_ref[1, top : top + rows, columns] = two
    position = (
        lax.broadcasted_iota(jnp.int32, (NBLK, tiles), 0) == place_ref[...]
    ).astype(jnp.float32)
    turns = jnp.dot(turns_ref[...], position, precision=precise, preferred_element_type=jnp.float32)
    cosine, sine = turns[: 2 * M], turns[2 * M :]
    near = math.exp(-0.5)
    turned = []
    for k in range(CYCLE_DEV):
        mixed = hist_ref[k] + near * hist_ref[1 - k]
        modes = jnp.dot(
            spectrum_ref[...], mixed, precision=precise, preferred_element_type=jnp.float32
        )
        turned.append(modes[: 2 * M] * cosine + modes[2 * M :] * sine)
    share = 2 * M // sky_count
    stacked = jnp.concatenate(
        [turned[k][z * share : (z + 1) * share] for z in range(sky_count) for k in range(CYCLE_DEV)],
        axis=0,
    )
    bins = SHELL_DEV * owners
    key = shell_ref[...] * owners + block_ref[...]
    hot = (lax.broadcasted_iota(jnp.int32, (bins, tiles), 0) == key).astype(jnp.float32)
    binned = lax.dot_general(
        hot, stacked, (((1,), (1,)), ((), ())), precision=precise, preferred_element_type=jnp.float32
    )
    width = CYCLE_DEV * share
    for z in range(sky_count):
        out_ref[z] = binned[:, z * width : (z + 1) * width]


def mode_kernel(
    counts, per, blocks, cycles, weight_ref, parts_ref, basis_ref, out_ref,
    halves, arrived, own_sem, half_send, half_recv, part_send, part_recv,
):
    shell_count, sky_count, sub_count = counts
    shell, sky, sub = lax.axis_index("shell"), lax.axis_index("sky"), lax.axis_index("sub")
    peers = shell_count * sky_count * sub_count
    me = (shell * sky_count + sky) * sub_count + sub
    degrees = halves.shape[2]
    orders = basis_ref.shape[0] // cycles

    def place(rank):
        return dict(
            shell=rank // (sky_count * sub_count),
            sky=rank // sub_count % sky_count,
            sub=rank % sub_count,
        )

    barrier = pltpu.get_barrier_semaphore()

    @pl.loop(1, peers)
    def _(j):
        pl.semaphore_signal(
            barrier, inc=1, device_id=place((me + j) % peers), device_id_type=MESH
        )

    pl.semaphore_wait(barrier, peers - 1)

    def send(j):
        target = place((me + j) % peers)
        return pltpu.make_async_remote_copy(
            src_ref=parts_ref.at[target["sky"]],
            dst_ref=arrived.at[me],
            send_sem=part_send.at[j],
            recv_sem=part_recv.at[j],
            device_id=target,
            device_id_type=MESH,
        )

    def expect(j):
        source = (me + peers - j) % peers
        return pltpu.make_async_remote_copy(
            src_ref=parts_ref.at[0],
            dst_ref=arrived.at[source],
            send_sem=part_send.at[j],
            recv_sem=part_recv.at[j],
            device_id=place(source),
            device_id_type=MESH,
        )

    @pl.loop(1, peers)
    def _(j):
        send(j).start()

    def half(j):
        target = (sub + j) % sub_count
        return pltpu.make_async_remote_copy(
            src_ref=basis_ref.at[:, pl.ds(pl.multiple_of(target * degrees, degrees), degrees)],
            dst_ref=halves.at[sub],
            send_sem=half_send.at[j],
            recv_sem=half_recv.at[j],
            device_id={"sub": target},
            device_id_type=MESH,
        )

    def expect_half(j):
        source = (sub + sub_count - j) % sub_count
        return pltpu.make_async_remote_copy(
            src_ref=basis_ref.at[:, pl.ds(0, degrees)],
            dst_ref=halves.at[source],
            send_sem=half_send.at[j],
            recv_sem=half_recv.at[j],
            device_id={"sub": source},
            device_id_type=MESH,
        )

    for j in range(1, sub_count):
        half(j).start()
    own = pltpu.make_async_copy(
        basis_ref.at[:, pl.ds(pl.multiple_of(sub * degrees, degrees), degrees)],
        halves.at[sub],
        own_sem,
    )
    own.start()
    arrived[me] = parts_ref[sky]

    @pl.loop(1, peers)
    def _(j):
        expect(j).wait_recv()

    group = sky_count * sub_count
    folded = [None] * per
    for x in range(shell_count):
        total = jnp.sum(arrived[x * group : (x + 1) * group], axis=0)
        modes = (total * (2.0 * math.pi / NP)).astype(jnp.bfloat16).astype(jnp.float32)
        for s in range(SHELL_DEV):
            part = modes[s * blocks : (s + 1) * blocks]
            lens = x * SHELL_DEV + s
            for i in range(per):
                source = shell * per + i
                weight = jnp.where(lens <= source, weight_ref[source, lens], 0.0)
                term = weight * part
                folded[i] = term if folded[i] is None else folded[i] + term
    coefficients = jnp.concatenate(folded, axis=0).T
    high = coefficients.astype(jnp.bfloat16)
    low = (coefficients - high.astype(jnp.float32)).astype(jnp.bfloat16)
    depth = orders * cycles
    span = 2 * orders
    lane = lax.broadcasted_iota(jnp.int32, (per * blocks, depth), 1)
    row = lax.broadcasted_iota(jnp.int32, (per * blocks, depth), 0)
    lane_out = lax.broadcasted_iota(jnp.int32, (span, depth), 1)
    diagonal = lane_out // cycles == lax.broadcasted_iota(jnp.int32, (span, depth), 0) // 2
    even = lane_out % CYCLE_DEV == 0
    left = []
    for h in range(sub_count):
        rows = []
        for piece in (high, low):
            for i in range(per):
                block = i * blocks + h * (cycles // CYCLE_DEV) + lane % cycles // CYCLE_DEV
                pick = (row == block).astype(jnp.float32).astype(jnp.bfloat16)
                spread = jnp.dot(piece, pick, preferred_element_type=jnp.float32)
                chosen = jnp.where(even, spread[:span], spread[span:])
                rows.append(jnp.where(diagonal, chosen, 0.0).astype(jnp.bfloat16))
        left.append(jnp.concatenate(rows, axis=0))
    own.wait()
    for j in range(1, sub_count):
        expect_half(j).wait_recv()
    step = 512
    for first in range(0, degrees, step):
        columns = slice(first, first + step)
        result = None
        for h in range(sub_count):
            term = jnp.dot(left[h], halves[h, :, columns], preferred_element_type=jnp.float32)
            result = term if result is None else result + term
        result = result[: per * span] + result[per * span :]
        for i in range(per):
            out_ref[i, :, columns] = result[i * span : (i + 1) * span]
    for j in range(1, sub_count):
        half(j).wait_send()

    @pl.loop(1, peers)
    def _(j):
        send(j).wait_send()


def body(
    part_cycle,
    part_pixel,
    part_mass,
    tile_block,
    tile_shell,
    tile_pixel,
    harmonic_basis,
    lens_weight,
):
    shell_count, sky_count, sub_count = (
        lax.axis_size("shell"),
        lax.axis_size("sky"),
        lax.axis_size("sub"),
    )
    owners = sky_count * sub_count
    peers = shell_count * owners
    tiles, particles = part_cycle.shape[1:]
    orders, cycles, degrees = harmonic_basis.shape
    per = lens_weight.shape[0] // shell_count
    share = degrees // sub_count
    bins = SHELL_DEV * owners
    width = 2 * CYCLE_DEV * orders
    spectrum, turns = tables()
    vmem = pl.BlockSpec(memory_space=pltpu.VMEM)
    parts = pl.pallas_call(
        functools.partial(deposit_kernel, sky_count, owners),
        out_shape=jax.ShapeDtypeStruct((sky_count, bins, width), jnp.float32),
        in_specs=[vmem] * 8,
        out_specs=vmem,
        scratch_shapes=[
            pltpu.VMEM((tiles // 128, particles, 128), jnp.int32),
            pltpu.VMEM((tiles // 128, particles, 128), jnp.float32),
            pltpu.VMEM((tiles // 128, particles, 128), jnp.float32),
            pltpu.VMEM((CYCLE_DEV, TP, tiles), jnp.float32),
        ],
        compiler_params=pltpu.CompilerParams(vmem_limit_bytes=24 << 20),
        name="deposit",
    )(
        part_cycle[0],
        part_pixel[0],
        part_mass[0],
        tile_block.reshape(1, tiles),
        tile_shell,
        tile_pixel,
        spectrum,
        turns,
    )
    result = pl.pallas_call(
        functools.partial(mode_kernel, (shell_count, sky_count, sub_count), per, owners, cycles),
        out_shape=jax.ShapeDtypeStruct((per, 2 * orders, share), jnp.float32),
        in_specs=[pl.BlockSpec(memory_space=pltpu.SMEM), vmem, pl.BlockSpec(memory_space=pl.ANY)],
        out_specs=vmem,
        scratch_shapes=[
            pltpu.VMEM((sub_count, orders * cycles, share), jnp.bfloat16),
            pltpu.VMEM((peers, bins, width), jnp.float32),
            pltpu.SemaphoreType.DMA,
            pltpu.SemaphoreType.DMA((sub_count,)),
            pltpu.SemaphoreType.DMA((sub_count,)),
            pltpu.SemaphoreType.DMA((peers,)),
            pltpu.SemaphoreType.DMA((peers,)),
        ],
        compiler_params=pltpu.CompilerParams(
            collective_id=0, has_side_effects=True, vmem_limit_bytes=24 << 20
        ),
        name="modes",
    )(lens_weight, parts, harmonic_basis.reshape(orders * cycles, degrees))
    return result.reshape(per, orders, 2, share)


def solution(mesh):
    return jax.shard_map(
        body,
        mesh=mesh,
        in_specs=(
            P("shell", ("sky", "sub"), None),
            P("shell", ("sky", "sub"), None),
            P("shell", ("sky", "sub"), None),
            P("shell", ("sky", "sub"), None),
            P("shell", ("sky", "sub")),
            P("shell", ("sky", "sub")),
            P("sky", "sub", None),
            P(),
        ),
        out_specs=P(("groups", "shell"), "sky", None, "sub"),
        check_vma=False,
    )
```

```python
import functools
import math

import jax
import jax.numpy as jnp
import numpy as np
from jax import lax
from jax.experimental import pallas as pl
from jax.experimental.pallas import tpu as pltpu
from jax.sharding import PartitionSpec as P

NP = 8192
M = 128
TP = 128
CYCLE_DEV = 2
SHELL_DEV = 2
NBLK = NP // TP

precise = lax.Precision.HIGHEST
MESH = pl.DeviceIdType.MESH


def tables():
    pixel = np.arange(TP, dtype=np.float64)
    smooth = np.exp(-((pixel[:, None] - pixel[None, :]) ** 2) / 18.0)
    orders = np.arange(M)
    angle = 2.0 * math.pi * ((np.arange(TP)[:, None] * orders[None, :]) % NP) / NP
    real, imag = smooth @ np.cos(angle), -(smooth @ np.sin(angle))
    straight = np.stack([real, imag], axis=2).reshape(TP, 2 * M).T
    crossed = np.stack([-imag, real], axis=2).reshape(TP, 2 * M).T
    turn = 2.0 * math.pi * ((np.arange(NBLK)[:, None] * TP * orders[None, :]) % NP) / NP
    cosine = np.repeat(np.cos(turn), 2, axis=1).T
    sine = np.repeat(-np.sin(turn), 2, axis=1).T
    spectrum = np.concatenate([straight, crossed], axis=0).astype(np.float32)
    turns = np.concatenate([cosine, sine], axis=0).astype(np.float32)
    return spectrum, turns


def deposit(
    sky_count, owners, cycle_ref, pixel_ref, mass_ref, block_ref, shell_ref, place_ref, spectrum_ref,
    turns_ref, out_ref, pixel_t, mass0_t, mass1_t, hist_ref, fetch_particles, fetch_tables, early,
):
    tiles, particles = pixel_ref.shape
    lanes = 128
    rows = 64
    fetch_particles()
    masses = mass_ref[...]
    first = cycle_ref[...] == 0
    for held, value in (
        (pixel_t, pixel_ref[...]),
        (mass0_t, jnp.where(first, masses, 0.0)),
        (mass1_t, jnp.where(first, 0.0, masses)),
    ):
        turned = value.T
        for side in range(tiles // lanes):
            held[side] = turned[:, side * lanes : (side + 1) * lanes]
    for side in range(tiles // lanes):
        columns = slice(side * lanes, (side + 1) * lanes)
        for top in range(0, TP, rows):
            ids = lax.broadcasted_iota(jnp.int32, (rows, lanes), 0) + top

            def step(p, sums):
                here = jnp.broadcast_to(pixel_t[side, pl.ds(p, 1), :], (rows, lanes)) == ids
                one = jnp.broadcast_to(mass0_t[side, pl.ds(p, 1), :], (rows, lanes))
                two = jnp.broadcast_to(mass1_t[side, pl.ds(p, 1), :], (rows, lanes))
                return sums[0] + jnp.where(here, one, 0.0), sums[1] + jnp.where(here, two, 0.0)

            zero = jnp.zeros((rows, lanes), jnp.float32)
            one, two = lax.fori_loop(0, particles, step, (zero, zero), unroll=8)
            if side == 0 and top == 0:
                early()
            hist_ref[0, top : top + rows, columns] = one
            hist_ref[1, top : top + rows, columns] = two
    fetch_tables()
    position = (
        lax.broadcasted_iota(jnp.int32, (NBLK, tiles), 0) == place_ref[...]
    ).astype(jnp.float32)
    turns = jnp.dot(turns_ref[...], position, precision=precise, preferred_element_type=jnp.float32)
    cosine, sine = turns[: 2 * M], turns[2 * M :]
    near = math.exp(-0.5)
    turned = []
    for k in range(CYCLE_DEV):
        mixed = hist_ref[k] + near * hist_ref[1 - k]
        modes = jnp.dot(
            spectrum_ref[...], mixed, precision=precise, preferred_element_type=jnp.float32
        )
        turned.append(modes[: 2 * M] * cosine + modes[2 * M :] * sine)
    share = 2 * M // sky_count
    stacked = jnp.concatenate(
        [turned[k][z * share : (z + 1) * share] for z in range(sky_count) for k in range(CYCLE_DEV)],
        axis=0,
    )
    bins = SHELL_DEV * owners
    key = shell_ref[...] * owners + block_ref[...]
    hot = (lax.broadcasted_iota(jnp.int32, (bins, tiles), 0) == key).astype(jnp.float32)
    binned = lax.dot_general(
        hot, stacked, (((1,), (1,)), ((), ())), precision=precise, preferred_element_type=jnp.float32
    )
    width = CYCLE_DEV * share
    for z in range(sky_count):
        out_ref[z] = binned[:, z * width : (z + 1) * width]


def kernel(
    counts, per, blocks, cycles, cycle_hbm, pixel_hbm, mass_hbm, block_hbm, shell_hbm, place_hbm,
    spectrum_hbm, turns_hbm, weight_hbm, basis_ref, out_ref,
    cycle_ref, pixel_ref, mass_ref, block_ref, shell_ref, place_ref, spectrum_ref, turns_ref,
    weight_ref, pixel_t, mass0_t, mass1_t, hist_ref, parts_ref,
    halves, arrived, fetch_sem, own_sem, half_send, half_recv, part_send, part_recv,
):
    fetches = [
        pltpu.make_async_copy(source, target, fetch_sem.at[n])
        for n, (source, target) in enumerate(
            (
                (cycle_hbm, cycle_ref),
                (pixel_hbm, pixel_ref),
                (mass_hbm, mass_ref),
                (spectrum_hbm, spectrum_ref),
                (turns_hbm, turns_ref),
                (block_hbm, block_ref),
                (shell_hbm, shell_ref),
                (place_hbm, place_ref),
                (weight_hbm, weight_ref),
            )
        )
    ]
    for fetch in fetches:
        fetch.start()
    shell_count, sky_count, sub_count = counts
    shell, sky, sub = lax.axis_index("shell"), lax.axis_index("sky"), lax.axis_index("sub")
    peers = shell_count * sky_count * sub_count
    me = (shell * sky_count + sky) * sub_count + sub
    degrees = halves.shape[2]
    orders = basis_ref.shape[0] // cycles

    def place(rank):
        return dict(
            shell=rank // (sky_count * sub_count),
            sky=rank // sub_count % sky_count,
            sub=rank % sub_count,
        )

    barrier = pltpu.get_barrier_semaphore()

    @pl.loop(1, peers)
    def _(j):
        pl.semaphore_signal(
            barrier, inc=1, device_id=place((me + j) % peers), device_id_type=MESH
        )

    def send(j):
        target = place((me + j) % peers)
        return pltpu.make_async_remote_copy(
            src_ref=parts_ref.at[target["sky"]],
            dst_ref=arrived.at[me],
            send_sem=part_send.at[j],
            recv_sem=part_recv.at[j],
            device_id=target,
            device_id_type=MESH,
        )

    def expect(j):
        source = (me + peers - j) % peers
        return pltpu.make_async_remote_copy(
            src_ref=parts_ref.at[0],
            dst_ref=arrived.at[source],
            send_sem=part_send.at[j],
            recv_sem=part_recv.at[j],
            device_id=place(source),
            device_id_type=MESH,
        )

    def half(j):
        target = (sub + j) % sub_count
        return pltpu.make_async_remote_copy(
            src_ref=basis_ref.at[:, pl.ds(pl.multiple_of(target * degrees, degrees), degrees)],
            dst_ref=halves.at[sub],
            send_sem=half_send.at[j],
            recv_sem=half_recv.at[j],
            device_id={"sub": target},
            device_id_type=MESH,
        )

    def expect_half(j):
        source = (sub + sub_count - j) % sub_count
        return pltpu.make_async_remote_copy(
            src_ref=basis_ref.at[:, pl.ds(0, degrees)],
            dst_ref=halves.at[source],
            send_sem=half_send.at[j],
            recv_sem=half_recv.at[j],
            device_id={"sub": source},
            device_id_type=MESH,
        )

    own = pltpu.make_async_copy(
        basis_ref.at[:, pl.ds(pl.multiple_of(sub * degrees, degrees), degrees)],
        halves.at[sub],
        own_sem,
    )
    own.start()

    def fetch_particles():
        for fetch in fetches[:3]:
            fetch.wait()

    def fetch_tables():
        for fetch in fetches[3:]:
            fetch.wait()

    def early():
        pl.semaphore_wait(barrier, peers - 1)
        for j in range(1, sub_count):
            half(j).start()

    deposit(
        sky_count, blocks, cycle_ref, pixel_ref, mass_ref, block_ref, shell_ref, place_ref,
        spectrum_ref, turns_ref, parts_ref, pixel_t, mass0_t, mass1_t, hist_ref,
        fetch_particles, fetch_tables, early,
    )

    @pl.loop(1, peers)
    def _(j):
        send(j).start()

    arrived[me] = parts_ref[sky]

    @pl.loop(1, peers)
    def _(j):
        expect(j).wait_recv()

    group = sky_count * sub_count
    folded = [None] * per
    for x in range(shell_count):
        total = jnp.sum(arrived[x * group : (x + 1) * group], axis=0)
        modes = (total * (2.0 * math.pi / NP)).astype(jnp.bfloat16).astype(jnp.float32)
        for s in range(SHELL_DEV):
            part = modes[s * blocks : (s + 1) * blocks]
            lens = x * SHELL_DEV + s
            for i in range(per):
                source = shell * per + i
                weight = jnp.where(lens <= source, weight_ref[source, lens], 0.0)
                term = weight * part
                folded[i] = term if folded[i] is None else folded[i] + term
    coefficients = jnp.concatenate(folded, axis=0).T
    high = coefficients.astype(jnp.bfloat16)
    low = (coefficients - high.astype(jnp.float32)).astype(jnp.bfloat16)
    depth = orders * cycles
    span = 2 * orders
    lane = lax.broadcasted_iota(jnp.int32, (per * blocks, depth), 1)
    row = lax.broadcasted_iota(jnp.int32, (per * blocks, depth), 0)
    lane_out = lax.broadcasted_iota(jnp.int32, (span, depth), 1)
    diagonal = lane_out // cycles == lax.broadcasted_iota(jnp.int32, (span, depth), 0) // 2
    even = lane_out % CYCLE_DEV == 0
    left = []
    for h in range(sub_count):
        rows = []
        for piece in (high, low):
            for i in range(per):
                block = i * blocks + h * (cycles // CYCLE_DEV) + lane % cycles // CYCLE_DEV
                pick = (row == block).astype(jnp.float32).astype(jnp.bfloat16)
                spread = jnp.dot(piece, pick, preferred_element_type=jnp.float32)
                chosen = jnp.where(even, spread[:span], spread[span:])
                rows.append(jnp.where(diagonal, chosen, 0.0).astype(jnp.bfloat16))
        left.append(jnp.concatenate(rows, axis=0))
    own.wait()
    for j in range(1, sub_count):
        expect_half(j).wait_recv()
    step = 512
    for first in range(0, degrees, step):
        columns = slice(first, first + step)
        result = None
        for h in range(sub_count):
            term = jnp.dot(left[h], halves[h, :, columns], preferred_element_type=jnp.float32)
            result = term if result is None else result + term
        result = result[: per * span] + result[per * span :]
        for i in range(per):
            out_ref[i, :, columns] = result[i * span : (i + 1) * span]
    for j in range(1, sub_count):
        half(j).wait_send()

    @pl.loop(1, peers)
    def _(j):
        send(j).wait_send()


def body(
    part_cycle,
    part_pixel,
    part_mass,
    tile_block,
    tile_shell,
    tile_pixel,
    harmonic_basis,
    lens_weight,
):
    shell_count, sky_count, sub_count = (
        lax.axis_size("shell"),
        lax.axis_size("sky"),
        lax.axis_size("sub"),
    )
    owners = sky_count * sub_count
    peers = shell_count * owners
    tiles, particles = part_cycle.shape[1:]
    orders, cycles, degrees = harmonic_basis.shape
    per = lens_weight.shape[0] // shell_count
    share = degrees // sub_count
    bins = SHELL_DEV * owners
    width = 2 * CYCLE_DEV * orders
    spectrum, turns = tables()
    result = pl.pallas_call(
        functools.partial(kernel, (shell_count, sky_count, sub_count), per, owners, cycles),
        out_shape=jax.ShapeDtypeStruct((per, 2 * orders, share), jnp.float32),
        in_specs=[pl.BlockSpec(memory_space=pltpu.HBM)] * 10,
        out_specs=pl.BlockSpec(memory_space=pltpu.VMEM),
        scratch_shapes=[
            pltpu.VMEM((tiles, particles), jnp.int32),
            pltpu.VMEM((tiles, particles), jnp.int32),
            pltpu.VMEM((tiles, particles), jnp.float32),
            pltpu.VMEM((1, tiles), jnp.int32),
            pltpu.VMEM((1, tiles), jnp.int32),
            pltpu.VMEM((1, tiles), jnp.int32),
            pltpu.VMEM(spectrum.shape, jnp.float32),
            pltpu.VMEM(turns.shape, jnp.float32),
            pltpu.SMEM(lens_weight.shape, jnp.float32),
            pltpu.VMEM((tiles // 128, particles, 128), jnp.int32),
            pltpu.VMEM((tiles // 128, particles, 128), jnp.float32),
            pltpu.VMEM((tiles // 128, particles, 128), jnp.float32),
            pltpu.VMEM((CYCLE_DEV, TP, tiles), jnp.float32),
            pltpu.VMEM((sky_count, bins, width), jnp.float32),
            pltpu.VMEM((sub_count, orders * cycles, share), jnp.bfloat16),
            pltpu.VMEM((peers, bins, width), jnp.float32),
            pltpu.SemaphoreType.DMA((9,)),
            pltpu.SemaphoreType.DMA,
            pltpu.SemaphoreType.DMA((sub_count,)),
            pltpu.SemaphoreType.DMA((sub_count,)),
            pltpu.SemaphoreType.DMA((peers,)),
            pltpu.SemaphoreType.DMA((peers,)),
        ],
        compiler_params=pltpu.CompilerParams(
            collective_id=0, has_side_effects=True, vmem_limit_bytes=60 << 20
        ),
        name="modes",
    )(
        part_cycle[0],
        part_pixel[0],
        part_mass[0],
        tile_block.reshape(1, tiles),
        tile_shell,
        tile_pixel,
        spectrum,
        turns,
        lens_weight,
        harmonic_basis.reshape(orders * cycles, degrees),
    )
    return result.reshape(per, orders, 2, share)


def solution(mesh):
    return jax.shard_map(
        body,
        mesh=mesh,
        in_specs=(
            P("shell", ("sky", "sub"), None),
            P("shell", ("sky", "sub"), None),
            P("shell", ("sky", "sub"), None),
            P("shell", ("sky", "sub"), None),
            P("shell", ("sky", "sub")),
            P("shell", ("sky", "sub")),
            P("sky", "sub", None),
            P(),
        ),
        out_specs=P(("groups", "shell"), "sky", None, "sub"),
        check_vma=False,
    )
```

```python
import functools
import math

import jax
import jax.numpy as jnp
import numpy as np
from jax import lax
from jax.experimental import pallas as pl
from jax.experimental.pallas import tpu as pltpu
from jax.sharding import PartitionSpec as P

NP = 8192
M = 128
TP = 128
CYCLE_DEV = 2
SHELL_DEV = 2
NBLK = NP // TP

MESH = pl.DeviceIdType.MESH


def tables():
    pixel = np.arange(TP, dtype=np.float64)
    smooth = np.exp(-((pixel[:, None] - pixel[None, :]) ** 2) / 18.0)
    orders = np.arange(M)
    angle = 2.0 * math.pi * ((np.arange(TP)[:, None] * orders[None, :]) % NP) / NP
    turn = 2.0 * math.pi * ((np.arange(NBLK)[:, None] * TP * orders[None, :]) % NP) / NP
    spectrum = np.concatenate([smooth @ np.cos(angle), -(smooth @ np.sin(angle))], axis=1)
    turns = np.concatenate([np.cos(turn), -np.sin(turn)], axis=1)

    def split(table):
        high = table.astype(jnp.bfloat16)
        low = (table - high.astype(np.float64)).astype(jnp.bfloat16)
        return np.concatenate([high, low], axis=0).astype(np.float32)

    return split(spectrum), split(turns)


def split(values):
    high = values.astype(jnp.bfloat16)
    return high, (values - high.astype(jnp.float32)).astype(jnp.bfloat16)


def dot(one, two, right=0):
    return lax.dot_general(
        one, two, (((1,), (right,)), ((), ())), preferred_element_type=jnp.float32
    )


FINE = 32
SIDE = 128


def deposit(
    sky_count, owners, cycle_ref, pixel_ref, mass_ref, block_ref, shell_ref, place_ref, spectrum_ref,
    turns_ref, out_ref, key_ref, fine_ref, high_ref, low_ref, hist_ref, fetch_particles, fetch_tables,
    early,
):
    halves, tiles = pixel_ref.shape[:2]
    coarse = TP // FINE
    bundle = 2 * SIDE // FINE
    groups = tiles // bundle
    keys = CYCLE_DEV * coarse
    fetch_particles()
    masses = mass_ref[...]
    pixels = pixel_ref[...]
    high = masses.astype(jnp.bfloat16).astype(jnp.float32)
    high_ref[...] = high
    low_ref[...] = masses - high
    fine_ref[...] = pixels % FINE
    key_ref[...] = cycle_ref[...] * coarse + pixels // FINE
    fine_ids = lax.broadcasted_iota(jnp.int32, (FINE, SIDE), 0)
    key_ids = lax.broadcasted_iota(jnp.int32, (keys, SIDE), 0)
    same = (
        lax.broadcasted_iota(jnp.int32, (bundle * keys, bundle * FINE), 0) // keys
        == lax.broadcasted_iota(jnp.int32, (bundle * keys, bundle * FINE), 1) // FINE
    )

    def group(g, carry):
        spread, highs, lows = [], [], []
        for t in range(bundle):
            row = pl.ds(t * groups + g, 1)
            spread_t, high_t, low_t = [], [], []
            for h in range(halves):
                fine = jnp.broadcast_to(fine_ref[h, row, :], (FINE, SIDE))
                spread_t.append(jnp.where(fine == fine_ids, 1.0, 0.0))
                here = jnp.broadcast_to(key_ref[h, row, :], (keys, SIDE)) == key_ids
                high_t.append(
                    jnp.where(here, jnp.broadcast_to(high_ref[h, row, :], (keys, SIDE)), 0.0)
                )
                low_t.append(
                    jnp.where(here, jnp.broadcast_to(low_ref[h, row, :], (keys, SIDE)), 0.0)
                )
            spread.append(jnp.concatenate(spread_t, axis=1).astype(jnp.bfloat16))
            highs.append(jnp.concatenate(high_t, axis=1))
            lows.append(jnp.concatenate(low_t, axis=1))
        weights = jnp.concatenate(highs + lows, axis=0).astype(jnp.bfloat16)
        pairs = dot(weights, jnp.concatenate(spread, axis=0), 1)
        count = bundle * keys
        pairs = jnp.where(same, pairs[:count] + pairs[count:], 0.0)
        own = jnp.sum(pairs.reshape(bundle, keys, bundle * FINE), axis=0)
        at = pl.ds(pl.multiple_of(g * keys, keys), keys)
        for side in range(bundle * FINE // SIDE):
            hist_ref[side, at, :] = own[:, side * SIDE : (side + 1) * SIDE]
        return carry

    lax.fori_loop(0, groups // 2, group, 0, unroll=4)
    early()
    lax.fori_loop(groups // 2, groups, group, 0, unroll=4)
    fetch_tables()
    lane = lax.broadcasted_iota(jnp.int32, (groups, SIDE), 1) // FINE
    strips = [
        [hist_ref[side, pl.ds(key, groups, stride=keys), :] for key in range(keys)]
        for side in range(bundle * FINE // SIDE)
    ]
    hist = []
    for c in range(CYCLE_DEV):
        for t in range(bundle):
            side, offset = t * FINE // SIDE, t * FINE % SIDE
            joined = None
            for x in range(coarse):
                shift = (x * FINE - offset) % SIDE
                strip = strips[side][c * coarse + x]
                moved = strip if shift == 0 else pltpu.roll(strip, shift, 1)
                joined = moved if joined is None else jnp.where(lane == x, moved, joined)
            hist.append(joined)
    high, low = split(jnp.concatenate(hist, axis=0))
    spectrum = spectrum_ref[...].astype(jnp.bfloat16)
    modes = dot(high, spectrum[:TP]) + dot(low, spectrum[:TP]) + dot(high, spectrum[TP:])
    position = lax.broadcasted_iota(jnp.int32, (2 * NBLK, tiles), 0) % NBLK == place_ref[...]
    position = jnp.where(position, 1.0, 0.0).T.astype(jnp.bfloat16)
    turns = dot(position, turns_ref[...].astype(jnp.bfloat16))
    cosine, sine = turns[:, :M], turns[:, M:]
    turned = []
    for c in range(CYCLE_DEV):
        real = modes[c * tiles : (c + 1) * tiles, :M]
        imag = modes[c * tiles : (c + 1) * tiles, M:]
        turned += [real * cosine - imag * sine, real * sine + imag * cosine]
    bins = SHELL_DEV * owners
    key = shell_ref[...] * owners + block_ref[...]
    hot = lax.broadcasted_iota(jnp.int32, (bins, tiles), 0) == key
    hot = jnp.where(hot, 1.0, 0.0).astype(jnp.bfloat16)
    high, low = split(jnp.concatenate(turned, axis=1))
    binned = dot(hot, high) + dot(hot, low)
    pieces = [binned[:, n * M : (n + 1) * M] for n in range(2 * CYCLE_DEV)]
    near = math.exp(-0.5)
    pieces = [
        pieces[2 * k + part] + near * pieces[2 * (1 - k) + part]
        for k in range(CYCLE_DEV)
        for part in range(2)
    ]
    share = M // sky_count
    width = len(pieces) * share
    lane = lax.broadcasted_iota(jnp.int32, (bins, M), 1) // share
    for z in range(sky_count):
        message = None
        for n, piece in enumerate(pieces):
            shift = (n - z) * share % M
            moved = piece if shift == 0 else pltpu.roll(piece, shift, 1)
            message = moved if message is None else jnp.where(lane == n, moved, message)
        out_ref[z] = message[:, :width]


def kernel(
    counts, per, blocks, cycles, cycle_hbm, pixel_hbm, mass_hbm, block_hbm, shell_hbm, place_hbm,
    spectrum_hbm, turns_hbm, weight_hbm, basis_ref, out_ref,
    cycle_ref, pixel_ref, mass_ref, block_ref, shell_ref, place_ref, spectrum_ref, turns_ref,
    weight_ref, key_ref, fine_ref, high_ref, low_ref, hist_ref, parts_ref,
    halves, arrived, fetch_sem, own_sem, half_send, half_recv, part_send, part_recv,
):
    fetches = [
        pltpu.make_async_copy(source, target, fetch_sem.at[n])
        for n, (source, target) in enumerate(
            (
                *(
                    (array.at[:, h * SIDE : (h + 1) * SIDE], held.at[h])
                    for array, held in (
                        (cycle_hbm, cycle_ref),
                        (pixel_hbm, pixel_ref),
                        (mass_hbm, mass_ref),
                    )
                    for h in range(cycle_ref.shape[0])
                ),
                (spectrum_hbm, spectrum_ref),
                (turns_hbm, turns_ref),
                (block_hbm, block_ref),
                (shell_hbm, shell_ref),
                (place_hbm, place_ref),
                (weight_hbm, weight_ref),
            )
        )
    ]
    for fetch in fetches:
        fetch.start()
    shell_count, sky_count, sub_count = counts
    shell, sky, sub = lax.axis_index("shell"), lax.axis_index("sky"), lax.axis_index("sub")
    peers = shell_count * sky_count * sub_count
    me = (shell * sky_count + sky) * sub_count + sub
    degrees = halves.shape[2]
    orders = basis_ref.shape[0] // cycles

    def place(rank):
        return dict(
            shell=rank // (sky_count * sub_count),
            sky=rank // sub_count % sky_count,
            sub=rank % sub_count,
        )

    barrier = pltpu.get_barrier_semaphore()

    @pl.loop(1, peers)
    def _(j):
        pl.semaphore_signal(
            barrier, inc=1, device_id=place((me + j) % peers), device_id_type=MESH
        )

    def send(j):
        target = place((me + j) % peers)
        return pltpu.make_async_remote_copy(
            src_ref=parts_ref.at[target["sky"]],
            dst_ref=arrived.at[me],
            send_sem=part_send.at[j],
            recv_sem=part_recv.at[j],
            device_id=target,
            device_id_type=MESH,
        )

    def expect(j):
        source = (me + peers - j) % peers
        return pltpu.make_async_remote_copy(
            src_ref=parts_ref.at[0],
            dst_ref=arrived.at[source],
            send_sem=part_send.at[j],
            recv_sem=part_recv.at[j],
            device_id=place(source),
            device_id_type=MESH,
        )

    def half(j):
        target = (sub + j) % sub_count
        return pltpu.make_async_remote_copy(
            src_ref=basis_ref.at[:, pl.ds(pl.multiple_of(target * degrees, degrees), degrees)],
            dst_ref=halves.at[sub],
            send_sem=half_send.at[j],
            recv_sem=half_recv.at[j],
            device_id={"sub": target},
            device_id_type=MESH,
        )

    def expect_half(j):
        source = (sub + sub_count - j) % sub_count
        return pltpu.make_async_remote_copy(
            src_ref=basis_ref.at[:, pl.ds(0, degrees)],
            dst_ref=halves.at[source],
            send_sem=half_send.at[j],
            recv_sem=half_recv.at[j],
            device_id={"sub": source},
            device_id_type=MESH,
        )

    own = pltpu.make_async_copy(
        basis_ref.at[:, pl.ds(pl.multiple_of(sub * degrees, degrees), degrees)],
        halves.at[sub],
        own_sem,
    )
    own.start()

    def fetch_particles():
        for fetch in fetches[:-6]:
            fetch.wait()

    def fetch_tables():
        for fetch in fetches[-6:]:
            fetch.wait()

    def early():
        pl.semaphore_wait(barrier, peers - 1)
        for j in range(1, sub_count):
            half(j).start()

    deposit(
        sky_count, blocks, cycle_ref, pixel_ref, mass_ref, block_ref, shell_ref, place_ref,
        spectrum_ref, turns_ref, parts_ref, key_ref, fine_ref, high_ref, low_ref, hist_ref,
        fetch_particles, fetch_tables, early,
    )

    @pl.loop(1, peers)
    def _(j):
        send(j).start()

    arrived[me] = parts_ref[sky]

    @pl.loop(1, peers)
    def _(j):
        expect(j).wait_recv()

    group = sky_count * sub_count
    folded = [None] * per
    for x in range(shell_count):
        total = jnp.sum(arrived[x * group : (x + 1) * group], axis=0)
        modes = (total * (2.0 * math.pi / NP)).astype(jnp.bfloat16).astype(jnp.float32)
        for s in range(SHELL_DEV):
            part = modes[s * blocks : (s + 1) * blocks]
            lens = x * SHELL_DEV + s
            for i in range(per):
                source = shell * per + i
                weight = jnp.where(lens <= source, weight_ref[source, lens], 0.0)
                term = weight * part
                folded[i] = term if folded[i] is None else folded[i] + term
    folded = jnp.concatenate(split(jnp.concatenate(folded, axis=0)), axis=0)
    width = folded.shape[1]
    to = lax.broadcasted_iota(jnp.int32, (width, width), 0)
    source = to // (2 * orders) * (2 * orders) + to % 2 * orders + to % (2 * orders) // 2
    swap = source == lax.broadcasted_iota(jnp.int32, (width, width), 1)
    swap = jnp.where(swap, 1.0, 0.0).astype(jnp.bfloat16)
    coefficients = dot(swap, folded, 1).astype(jnp.bfloat16)
    depth = orders * cycles
    span = 2 * orders
    lane = lax.broadcasted_iota(jnp.int32, (2 * per * blocks, depth), 1)
    row = lax.broadcasted_iota(jnp.int32, (2 * per * blocks, depth), 0)
    lane_out = lax.broadcasted_iota(jnp.int32, (span, depth), 1)
    diagonal = lane_out // cycles == lax.broadcasted_iota(jnp.int32, (span, depth), 0) // 2
    even = lane_out % CYCLE_DEV == 0
    left = []
    for h in range(sub_count):
        rows = []
        for piece in range(2):
            for i in range(per):
                block = (piece * per + i) * blocks + h * (cycles // CYCLE_DEV) + lane % cycles // CYCLE_DEV
                pick = jnp.where(row == block, 1.0, 0.0).astype(jnp.bfloat16)
                spread = dot(coefficients, pick)
                chosen = jnp.where(even, spread[:span], spread[span:])
                rows.append(jnp.where(diagonal, chosen, 0.0).astype(jnp.bfloat16))
        left.append(jnp.concatenate(rows, axis=0))
    own.wait()
    for j in range(1, sub_count):
        expect_half(j).wait_recv()
    step = 512
    for first in range(0, degrees, step):
        columns = slice(first, first + step)
        result = None
        for h in range(sub_count):
            term = jnp.dot(left[h], halves[h, :, columns], preferred_element_type=jnp.float32)
            result = term if result is None else result + term
        result = result[: per * span] + result[per * span :]
        for i in range(per):
            out_ref[i, :, :, columns] = result[i * span : (i + 1) * span].reshape(orders, 2, step)
    for j in range(1, sub_count):
        half(j).wait_send()

    @pl.loop(1, peers)
    def _(j):
        send(j).wait_send()


def body(
    part_cycle,
    part_pixel,
    part_mass,
    tile_block,
    tile_shell,
    tile_pixel,
    harmonic_basis,
    lens_weight,
):
    shell_count, sky_count, sub_count = (
        lax.axis_size("shell"),
        lax.axis_size("sky"),
        lax.axis_size("sub"),
    )
    owners = sky_count * sub_count
    peers = shell_count * owners
    tiles, particles = part_cycle.shape[1:]
    orders, cycles, degrees = harmonic_basis.shape
    per = lens_weight.shape[0] // shell_count
    share = degrees // sub_count
    bins = SHELL_DEV * owners
    width = 2 * CYCLE_DEV * orders
    spectrum, turns = tables()
    result = pl.pallas_call(
        functools.partial(kernel, (shell_count, sky_count, sub_count), per, owners, cycles),
        out_shape=pltpu.VMEM((per, orders, 2, share), jnp.float32),
        in_specs=[pl.BlockSpec(memory_space=pltpu.HBM)] * 10,
        out_specs=pl.BlockSpec(memory_space=pltpu.VMEM),
        scratch_shapes=[
            pltpu.VMEM((particles // SIDE, tiles, SIDE), jnp.int32),
            pltpu.VMEM((particles // SIDE, tiles, SIDE), jnp.int32),
            pltpu.VMEM((particles // SIDE, tiles, SIDE), jnp.float32),
            pltpu.VMEM((1, tiles), jnp.int32),
            pltpu.VMEM((1, tiles), jnp.int32),
            pltpu.VMEM((1, tiles), jnp.int32),
            pltpu.VMEM(spectrum.shape, jnp.float32),
            pltpu.VMEM(turns.shape, jnp.float32),
            pltpu.SMEM(lens_weight.shape, jnp.float32),
            pltpu.VMEM((particles // SIDE, tiles, SIDE), jnp.int32),
            pltpu.VMEM((particles // SIDE, tiles, SIDE), jnp.int32),
            pltpu.VMEM((particles // SIDE, tiles, SIDE), jnp.float32),
            pltpu.VMEM((particles // SIDE, tiles, SIDE), jnp.float32),
            pltpu.VMEM((2, tiles * CYCLE_DEV * TP // (2 * SIDE), SIDE), jnp.float32),
            pltpu.VMEM((sky_count, bins, width), jnp.float32),
            pltpu.VMEM((sub_count, orders * cycles, share), jnp.bfloat16),
            pltpu.VMEM((peers, bins, width), jnp.float32),
            pltpu.SemaphoreType.DMA((3 * (particles // SIDE) + 6,)),
            pltpu.SemaphoreType.DMA,
            pltpu.SemaphoreType.DMA((sub_count,)),
            pltpu.SemaphoreType.DMA((sub_count,)),
            pltpu.SemaphoreType.DMA((peers,)),
            pltpu.SemaphoreType.DMA((peers,)),
        ],
        compiler_params=pltpu.CompilerParams(
            collective_id=0, has_side_effects=True, vmem_limit_bytes=60 << 20
        ),
        name="modes",
    )(
        part_cycle[0],
        part_pixel[0],
        part_mass[0],
        tile_block.reshape(1, tiles),
        tile_shell,
        tile_pixel,
        spectrum,
        turns,
        lens_weight,
        harmonic_basis.reshape(orders * cycles, degrees),
    )
    return result


def solution(mesh):
    return jax.shard_map(
        body,
        mesh=mesh,
        in_specs=(
            P("shell", ("sky", "sub"), None),
            P("shell", ("sky", "sub"), None),
            P("shell", ("sky", "sub"), None),
            P("shell", ("sky", "sub"), None),
            P("shell", ("sky", "sub")),
            P("shell", ("sky", "sub")),
            P("sky", "sub", None),
            P(),
        ),
        out_specs=P(("groups", "shell"), "sky", None, "sub"),
        check_vma=False,
    )
```

```python
import functools
import math

import jax
import jax.numpy as jnp
import numpy as np
from jax import lax
from jax.experimental import pallas as pl
from jax.experimental.pallas import tpu as pltpu
from jax.sharding import PartitionSpec as P

NP = 8192
M = 128
TP = 128
CYCLE_DEV = 2
SHELL_DEV = 2
NBLK = NP // TP

MESH = pl.DeviceIdType.MESH


def tables():
    pixel = np.arange(TP, dtype=np.float64)
    smooth = np.exp(-((pixel[:, None] - pixel[None, :]) ** 2) / 18.0)
    orders = np.arange(M)
    angle = 2.0 * math.pi * ((np.arange(TP)[:, None] * orders[None, :]) % NP) / NP
    turn = 2.0 * math.pi * ((np.arange(NBLK)[:, None] * TP * orders[None, :]) % NP) / NP
    spectrum = np.concatenate([smooth @ np.cos(angle), -(smooth @ np.sin(angle))], axis=1)
    turns = np.concatenate([np.cos(turn), -np.sin(turn)], axis=1)

    def split(table):
        high = table.astype(jnp.bfloat16)
        low = (table - high.astype(np.float64)).astype(jnp.bfloat16)
        return np.concatenate([high, low], axis=0).astype(np.float32)

    return split(spectrum), split(turns)


def split(values):
    high = values.astype(jnp.bfloat16)
    return high, (values - high.astype(jnp.float32)).astype(jnp.bfloat16)


def dot(one, two, right=0):
    return lax.dot_general(
        one, two, (((1,), (right,)), ((), ())), preferred_element_type=jnp.float32
    )


FINE = 32
SIDE = 128


def quotient(value, by):
    return value >> (by.bit_length() - 1) if by & (by - 1) == 0 else value // by


def rest(value, by):
    return value & (by - 1) if by & (by - 1) == 0 else value % by


def deposit(
    sky_count, owners, cycle_ref, pixel_ref, mass_ref, block_ref, shell_ref, place_ref, spectrum_ref,
    turns_ref, out_ref, key_ref, fine_ref, high_ref, low_ref, hist_ref, fetch_particles, fetch_tables,
    early,
):
    halves, tiles = pixel_ref.shape[:2]
    coarse = TP // FINE
    bundle = 2 * SIDE // FINE
    groups = tiles // bundle
    keys = CYCLE_DEV * coarse
    fetch_particles()
    masses = mass_ref[...]
    pixels = pixel_ref[...]
    high = masses.astype(jnp.bfloat16).astype(jnp.float32)
    high_ref[...] = high
    low_ref[...] = masses - high
    fine_ref[...] = rest(pixels, FINE)
    key_ref[...] = cycle_ref[...] * coarse + quotient(pixels, FINE)
    fine_ids = lax.broadcasted_iota(jnp.int32, (FINE, SIDE), 0)
    key_ids = lax.broadcasted_iota(jnp.int32, (keys, SIDE), 0)
    same = (
        quotient(lax.broadcasted_iota(jnp.int32, (bundle * keys, bundle * FINE), 0), keys)
        == quotient(lax.broadcasted_iota(jnp.int32, (bundle * keys, bundle * FINE), 1), FINE)
    )

    def group(g, carry):
        spread, highs, lows = [], [], []
        for t in range(bundle):
            row = pl.ds(t * groups + g, 1)
            spread_t, high_t, low_t = [], [], []
            for h in range(halves):
                fine = jnp.broadcast_to(fine_ref[h, row, :], (FINE, SIDE))
                spread_t.append(jnp.where(fine == fine_ids, 1.0, 0.0))
                here = jnp.broadcast_to(key_ref[h, row, :], (keys, SIDE)) == key_ids
                high_t.append(
                    jnp.where(here, jnp.broadcast_to(high_ref[h, row, :], (keys, SIDE)), 0.0)
                )
                low_t.append(
                    jnp.where(here, jnp.broadcast_to(low_ref[h, row, :], (keys, SIDE)), 0.0)
                )
            spread.append(jnp.concatenate(spread_t, axis=1).astype(jnp.bfloat16))
            highs.append(jnp.concatenate(high_t, axis=1))
            lows.append(jnp.concatenate(low_t, axis=1))
        weights = jnp.concatenate(highs + lows, axis=0).astype(jnp.bfloat16)
        pairs = dot(weights, jnp.concatenate(spread, axis=0), 1)
        count = bundle * keys
        pairs = jnp.where(same, pairs[:count] + pairs[count:], 0.0)
        own = jnp.sum(pairs.reshape(bundle, keys, bundle * FINE), axis=0)
        at = pl.ds(pl.multiple_of(g * keys, keys), keys)
        for side in range(bundle * FINE // SIDE):
            hist_ref[side, at, :] = own[:, side * SIDE : (side + 1) * SIDE]
        return carry

    lax.fori_loop(0, groups // 2, group, 0, unroll=4)
    early()
    lax.fori_loop(groups // 2, groups, group, 0, unroll=4)
    fetch_tables()
    lane = quotient(lax.broadcasted_iota(jnp.int32, (groups, SIDE), 1), FINE)
    strips = [
        [hist_ref[side, pl.ds(key, groups, stride=keys), :] for key in range(keys)]
        for side in range(bundle * FINE // SIDE)
    ]
    hist = []
    for c in range(CYCLE_DEV):
        for t in range(bundle):
            side, offset = t * FINE // SIDE, t * FINE % SIDE
            joined = None
            for x in range(coarse):
                shift = (x * FINE - offset) % SIDE
                strip = strips[side][c * coarse + x]
                moved = strip if shift == 0 else pltpu.roll(strip, shift, 1)
                joined = moved if joined is None else jnp.where(lane == x, moved, joined)
            hist.append(joined)
    high, low = split(jnp.concatenate(hist, axis=0))
    spectrum = spectrum_ref[...].astype(jnp.bfloat16)
    modes = dot(high, spectrum[:TP]) + dot(low, spectrum[:TP]) + dot(high, spectrum[TP:])
    position = rest(lax.broadcasted_iota(jnp.int32, (2 * NBLK, tiles), 0), NBLK) == place_ref[...]
    position = jnp.where(position, 1.0, 0.0).T.astype(jnp.bfloat16)
    turns = dot(position, turns_ref[...].astype(jnp.bfloat16))
    cosine, sine = turns[:, :M], turns[:, M:]
    turned = []
    for c in range(CYCLE_DEV):
        real = modes[c * tiles : (c + 1) * tiles, :M]
        imag = modes[c * tiles : (c + 1) * tiles, M:]
        turned += [real * cosine - imag * sine, real * sine + imag * cosine]
    bins = SHELL_DEV * owners
    key = shell_ref[...] * owners + block_ref[...]
    hot = lax.broadcasted_iota(jnp.int32, (bins, tiles), 0) == key
    hot = jnp.where(hot, 1.0, 0.0).astype(jnp.bfloat16)
    high, low = split(jnp.concatenate(turned, axis=1))
    binned = dot(hot, high) + dot(hot, low)
    pieces = [binned[:, n * M : (n + 1) * M] for n in range(2 * CYCLE_DEV)]
    near = math.exp(-0.5)
    pieces = [
        pieces[2 * k + part] + near * pieces[2 * (1 - k) + part]
        for k in range(CYCLE_DEV)
        for part in range(2)
    ]
    share = M // sky_count
    width = len(pieces) * share
    lane = quotient(lax.broadcasted_iota(jnp.int32, (bins, M), 1), share)
    for z in range(sky_count):
        message = None
        for n, piece in enumerate(pieces):
            shift = (n - z) * share % M
            moved = piece if shift == 0 else pltpu.roll(piece, shift, 1)
            message = moved if message is None else jnp.where(lane == n, moved, message)
        out_ref[z] = message[:, :width]


def kernel(
    counts, per, blocks, cycles, cycle_hbm, pixel_hbm, mass_hbm, block_hbm, shell_hbm, place_hbm,
    spectrum_hbm, turns_hbm, weight_hbm, basis_ref, out_ref,
    cycle_ref, pixel_ref, mass_ref, block_ref, shell_ref, place_ref, spectrum_ref, turns_ref,
    weight_ref, key_ref, fine_ref, high_ref, low_ref, hist_ref, parts_ref,
    halves, arrived, fetch_sem, own_sem, half_send, half_recv, part_send, part_recv,
):
    fetches = [
        pltpu.make_async_copy(source, target, fetch_sem.at[n])
        for n, (source, target) in enumerate(
            (
                *(
                    (array.at[:, h * SIDE : (h + 1) * SIDE], held.at[h])
                    for array, held in (
                        (cycle_hbm, cycle_ref),
                        (pixel_hbm, pixel_ref),
                        (mass_hbm, mass_ref),
                    )
                    for h in range(cycle_ref.shape[0])
                ),
                (spectrum_hbm, spectrum_ref),
                (turns_hbm, turns_ref),
                (block_hbm, block_ref),
                (shell_hbm, shell_ref),
                (place_hbm, place_ref),
                (weight_hbm, weight_ref),
            )
        )
    ]
    for fetch in fetches:
        fetch.start()
    shell_count, sky_count, sub_count = counts
    shell, sky, sub = lax.axis_index("shell"), lax.axis_index("sky"), lax.axis_index("sub")
    peers = shell_count * sky_count * sub_count
    me = (shell * sky_count + sky) * sub_count + sub
    degrees = halves.shape[2]
    orders = basis_ref.shape[0] // cycles

    def place(rank):
        return dict(
            shell=quotient(rank, sky_count * sub_count),
            sky=rest(quotient(rank, sub_count), sky_count),
            sub=rest(rank, sub_count),
        )

    barrier = pltpu.get_barrier_semaphore()

    @pl.loop(1, peers, unroll=peers <= 16)
    def _(j):
        pl.semaphore_signal(
            barrier, inc=1, device_id=place(rest(me + j, peers)), device_id_type=MESH
        )

    def send(j):
        target = place(rest(me + j, peers))
        return pltpu.make_async_remote_copy(
            src_ref=parts_ref.at[target["sky"]],
            dst_ref=arrived.at[me],
            send_sem=part_send.at[j],
            recv_sem=part_recv.at[j],
            device_id=target,
            device_id_type=MESH,
        )

    def expect(j):
        source = rest(me + peers - j, peers)
        return pltpu.make_async_remote_copy(
            src_ref=parts_ref.at[0],
            dst_ref=arrived.at[source],
            send_sem=part_send.at[j],
            recv_sem=part_recv.at[j],
            device_id=place(source),
            device_id_type=MESH,
        )

    def half(j):
        target = rest(sub + j, sub_count)
        return pltpu.make_async_remote_copy(
            src_ref=basis_ref.at[:, pl.ds(pl.multiple_of(target * degrees, degrees), degrees)],
            dst_ref=halves.at[sub],
            send_sem=half_send.at[j],
            recv_sem=half_recv.at[j],
            device_id={"sub": target},
            device_id_type=MESH,
        )

    def expect_half(j):
        source = rest(sub + sub_count - j, sub_count)
        return pltpu.make_async_remote_copy(
            src_ref=basis_ref.at[:, pl.ds(0, degrees)],
            dst_ref=halves.at[source],
            send_sem=half_send.at[j],
            recv_sem=half_recv.at[j],
            device_id={"sub": source},
            device_id_type=MESH,
        )

    own = pltpu.make_async_copy(
        basis_ref.at[:, pl.ds(pl.multiple_of(sub * degrees, degrees), degrees)],
        halves.at[sub],
        own_sem,
    )
    own.start()

    def fetch_particles():
        for fetch in fetches[:-6]:
            fetch.wait()

    def fetch_tables():
        for fetch in fetches[-6:]:
            fetch.wait()

    def early():
        pl.semaphore_wait(barrier, peers - 1)
        for j in range(1, sub_count):
            half(j).start()

    deposit(
        sky_count, blocks, cycle_ref, pixel_ref, mass_ref, block_ref, shell_ref, place_ref,
        spectrum_ref, turns_ref, parts_ref, key_ref, fine_ref, high_ref, low_ref, hist_ref,
        fetch_particles, fetch_tables, early,
    )

    @pl.loop(1, peers, unroll=peers <= 16)
    def _(j):
        send(j).start()

    arrived[me] = parts_ref[sky]

    @pl.loop(1, peers, unroll=peers <= 16)
    def _(j):
        expect(j).wait_recv()

    group = sky_count * sub_count
    folded = [None] * per
    for x in range(shell_count):
        total = jnp.sum(arrived[x * group : (x + 1) * group], axis=0)
        modes = (total * (2.0 * math.pi / NP)).astype(jnp.bfloat16).astype(jnp.float32)
        for s in range(SHELL_DEV):
            part = modes[s * blocks : (s + 1) * blocks]
            lens = x * SHELL_DEV + s
            for i in range(per):
                source = shell * per + i
                weight = jnp.where(lens <= source, weight_ref[source, lens], 0.0)
                term = weight * part
                folded[i] = term if folded[i] is None else folded[i] + term
    folded = jnp.concatenate(split(jnp.concatenate(folded, axis=0)), axis=0)
    width = folded.shape[1]
    to = lax.broadcasted_iota(jnp.int32, (width, width), 0)
    within = rest(to, 2 * orders)
    source = to - within + rest(to, 2) * orders + quotient(within, 2)
    swap = source == lax.broadcasted_iota(jnp.int32, (width, width), 1)
    swap = jnp.where(swap, 1.0, 0.0).astype(jnp.bfloat16)
    coefficients = dot(swap, folded, 1).astype(jnp.bfloat16)
    depth = orders * cycles
    span = 2 * orders
    lane = lax.broadcasted_iota(jnp.int32, (2 * per * blocks, depth), 1)
    row = lax.broadcasted_iota(jnp.int32, (2 * per * blocks, depth), 0)
    lane_out = lax.broadcasted_iota(jnp.int32, (span, depth), 1)
    diagonal = quotient(lane_out, cycles) == quotient(
        lax.broadcasted_iota(jnp.int32, (span, depth), 0), 2
    )
    even = rest(lane_out, CYCLE_DEV) == 0
    turn = quotient(rest(lane, cycles), CYCLE_DEV)
    left = []
    for h in range(sub_count):
        rows = []
        for piece in range(2):
            for i in range(per):
                block = (piece * per + i) * blocks + h * (cycles // CYCLE_DEV) + turn
                pick = jnp.where(row == block, 1.0, 0.0).astype(jnp.bfloat16)
                spread = dot(coefficients, pick)
                chosen = jnp.where(even, spread[:span], spread[span:])
                rows.append(jnp.where(diagonal, chosen, 0.0).astype(jnp.bfloat16))
        left.append(jnp.concatenate(rows, axis=0))
    own.wait()
    for j in range(1, sub_count):
        expect_half(j).wait_recv()
    step = 512
    for first in range(0, degrees, step):
        columns = slice(first, first + step)
        result = None
        for h in range(sub_count):
            term = jnp.dot(left[h], halves[h, :, columns], preferred_element_type=jnp.float32)
            result = term if result is None else result + term
        result = result[: per * span] + result[per * span :]
        for i in range(per):
            out_ref[i, :, :, columns] = result[i * span : (i + 1) * span].reshape(orders, 2, step)
    for j in range(1, sub_count):
        half(j).wait_send()

    @pl.loop(1, peers, unroll=peers <= 16)
    def _(j):
        send(j).wait_send()


def body(
    part_cycle,
    part_pixel,
    part_mass,
    tile_block,
    tile_shell,
    tile_pixel,
    harmonic_basis,
    lens_weight,
):
    shell_count, sky_count, sub_count = (
        lax.axis_size("shell"),
        lax.axis_size("sky"),
        lax.axis_size("sub"),
    )
    owners = sky_count * sub_count
    peers = shell_count * owners
    tiles, particles = part_cycle.shape[1:]
    orders, cycles, degrees = harmonic_basis.shape
    per = lens_weight.shape[0] // shell_count
    share = degrees // sub_count
    bins = SHELL_DEV * owners
    width = 2 * CYCLE_DEV * orders
    spectrum, turns = tables()
    result = pl.pallas_call(
        functools.partial(kernel, (shell_count, sky_count, sub_count), per, owners, cycles),
        out_shape=pltpu.VMEM((per, orders, 2, share), jnp.float32),
        in_specs=[pl.BlockSpec(memory_space=pltpu.HBM)] * 10,
        out_specs=pl.BlockSpec(memory_space=pltpu.VMEM),
        scratch_shapes=[
            pltpu.VMEM((particles // SIDE, tiles, SIDE), jnp.int32),
            pltpu.VMEM((particles // SIDE, tiles, SIDE), jnp.int32),
            pltpu.VMEM((particles // SIDE, tiles, SIDE), jnp.float32),
            pltpu.VMEM((1, tiles), jnp.int32),
            pltpu.VMEM((1, tiles), jnp.int32),
            pltpu.VMEM((1, tiles), jnp.int32),
            pltpu.VMEM(spectrum.shape, jnp.float32),
            pltpu.VMEM(turns.shape, jnp.float32),
            pltpu.SMEM(lens_weight.shape, jnp.float32),
            pltpu.VMEM((particles // SIDE, tiles, SIDE), jnp.int32),
            pltpu.VMEM((particles // SIDE, tiles, SIDE), jnp.int32),
            pltpu.VMEM((particles // SIDE, tiles, SIDE), jnp.float32),
            pltpu.VMEM((particles // SIDE, tiles, SIDE), jnp.float32),
            pltpu.VMEM((2, tiles * CYCLE_DEV * TP // (2 * SIDE), SIDE), jnp.float32),
            pltpu.VMEM((sky_count, bins, width), jnp.float32),
            pltpu.VMEM((sub_count, orders * cycles, share), jnp.bfloat16),
            pltpu.VMEM((peers, bins, width), jnp.float32),
            pltpu.SemaphoreType.DMA((3 * (particles // SIDE) + 6,)),
            pltpu.SemaphoreType.DMA,
            pltpu.SemaphoreType.DMA((sub_count,)),
            pltpu.SemaphoreType.DMA((sub_count,)),
            pltpu.SemaphoreType.DMA((peers,)),
            pltpu.SemaphoreType.DMA((peers,)),
        ],
        compiler_params=pltpu.CompilerParams(
            collective_id=0, has_side_effects=True, vmem_limit_bytes=60 << 20
        ),
        name="modes",
    )(
        part_cycle[0],
        part_pixel[0],
        part_mass[0],
        tile_block.reshape(1, tiles),
        tile_shell,
        tile_pixel,
        spectrum,
        turns,
        lens_weight,
        harmonic_basis.reshape(orders * cycles, degrees),
    )
    return result


def solution(mesh):
    return jax.shard_map(
        body,
        mesh=mesh,
        in_specs=(
            P("shell", ("sky", "sub"), None),
            P("shell", ("sky", "sub"), None),
            P("shell", ("sky", "sub"), None),
            P("shell", ("sky", "sub"), None),
            P("shell", ("sky", "sub")),
            P("shell", ("sky", "sub")),
            P("sky", "sub", None),
            P(),
        ),
        out_specs=P(("groups", "shell"), "sky", None, "sub"),
        check_vma=False,
    )
```

```python
import functools
import math

import jax
import jax.numpy as jnp
import numpy as np
from jax import lax
from jax.experimental import pallas as pl
from jax.experimental.pallas import tpu as pltpu
from jax.sharding import PartitionSpec as P

NP = 8192
M = 128
TP = 128
CYCLE_DEV = 2
SHELL_DEV = 2
NBLK = NP // TP

MESH = pl.DeviceIdType.MESH


def tables():
    pixel = np.arange(TP, dtype=np.float64)
    smooth = np.exp(-((pixel[:, None] - pixel[None, :]) ** 2) / 18.0)
    orders = np.arange(M)
    angle = 2.0 * math.pi * ((np.arange(TP)[:, None] * orders[None, :]) % NP) / NP
    turn = 2.0 * math.pi * ((np.arange(NBLK)[:, None] * TP * orders[None, :]) % NP) / NP
    spectrum = np.concatenate([smooth @ np.cos(angle), -(smooth @ np.sin(angle))], axis=1)
    turns = np.concatenate([np.cos(turn), -np.sin(turn)], axis=1)

    def split(table):
        high = table.astype(jnp.bfloat16)
        low = (table - high.astype(np.float64)).astype(jnp.bfloat16)
        return np.concatenate([high, low], axis=0).astype(np.float32)

    return split(spectrum), split(turns)


def split(values):
    high = values.astype(jnp.bfloat16)
    return high, (values - high.astype(jnp.float32)).astype(jnp.bfloat16)


def dot(one, two, right=0):
    return lax.dot_general(
        one, two, (((1,), (right,)), ((), ())), preferred_element_type=jnp.float32
    )


FINE = 32
SIDE = 128


def quotient(value, by):
    return value >> (by.bit_length() - 1) if by & (by - 1) == 0 else value // by


def rest(value, by):
    return value & (by - 1) if by & (by - 1) == 0 else value % by


def deposit(
    sky_count, owners, cycle_ref, pixel_ref, mass_ref, block_ref, shell_ref, place_ref, spectrum_ref,
    turns_ref, out_ref, key_ref, fine_ref, high_ref, low_ref, hist_ref, fetch_particles, fetch_tables,
    early,
):
    halves, tiles = pixel_ref.shape[:2]
    coarse = TP // FINE
    bundle = 2 * SIDE // FINE
    groups = tiles // bundle
    keys = CYCLE_DEV * coarse
    fetch_particles()
    masses = mass_ref[...]
    pixels = pixel_ref[...]
    high = masses.astype(jnp.bfloat16).astype(jnp.float32)
    high_ref[...] = high
    low_ref[...] = masses - high
    fine_ref[...] = rest(pixels, FINE).astype(jnp.float32)
    key_ref[...] = cycle_ref[...] * coarse + quotient(pixels, FINE)
    fine_ids = lax.broadcasted_iota(jnp.int32, (FINE, SIDE), 0)
    fine_ids = fine_ids.astype(jnp.float32).astype(jnp.bfloat16)
    ones, zeros = jnp.ones((FINE, SIDE), jnp.bfloat16), jnp.zeros((FINE, SIDE), jnp.bfloat16)
    key_ids = lax.broadcasted_iota(jnp.int32, (keys, SIDE), 0)
    same = (
        quotient(lax.broadcasted_iota(jnp.int32, (bundle * keys, bundle * FINE), 0), keys)
        == quotient(lax.broadcasted_iota(jnp.int32, (bundle * keys, bundle * FINE), 1), FINE)
    )

    def group(g, carry):
        spread, highs, lows = [], [], []
        for t in range(bundle):
            row = pl.ds(t * groups + g, 1)
            spread_t, high_t, low_t = [], [], []
            for h in range(halves):
                fine = jnp.broadcast_to(fine_ref[h, row, :], (FINE, SIDE)).astype(jnp.bfloat16)
                spread_t.append(jnp.where(fine == fine_ids, ones, zeros))
                here = jnp.broadcast_to(key_ref[h, row, :], (keys, SIDE)) == key_ids
                high_t.append(
                    jnp.where(here, jnp.broadcast_to(high_ref[h, row, :], (keys, SIDE)), 0.0)
                )
                low_t.append(
                    jnp.where(here, jnp.broadcast_to(low_ref[h, row, :], (keys, SIDE)), 0.0)
                )
            spread.append(jnp.concatenate(spread_t, axis=1))
            highs.append(jnp.concatenate(high_t, axis=1))
            lows.append(jnp.concatenate(low_t, axis=1))
        weights = jnp.concatenate(highs + lows, axis=0).astype(jnp.bfloat16)
        pairs = dot(weights, jnp.concatenate(spread, axis=0), 1)
        count = bundle * keys
        pairs = jnp.where(same, pairs[:count] + pairs[count:], 0.0)
        own = jnp.sum(pairs.reshape(bundle, keys, bundle * FINE), axis=0)
        at = pl.ds(pl.multiple_of(g * keys, keys), keys)
        for side in range(bundle * FINE // SIDE):
            hist_ref[side, at, :] = own[:, side * SIDE : (side + 1) * SIDE]
        return carry

    lax.fori_loop(0, groups // 2, group, 0, unroll=4)
    early()
    lax.fori_loop(groups // 2, groups, group, 0, unroll=4)
    fetch_tables()
    lane = quotient(lax.broadcasted_iota(jnp.int32, (groups, SIDE), 1), FINE)
    strips = [
        [hist_ref[side, pl.ds(key, groups, stride=keys), :] for key in range(keys)]
        for side in range(bundle * FINE // SIDE)
    ]
    hist = []
    for c in range(CYCLE_DEV):
        for t in range(bundle):
            side, offset = t * FINE // SIDE, t * FINE % SIDE
            joined = None
            for x in range(coarse):
                shift = (x * FINE - offset) % SIDE
                strip = strips[side][c * coarse + x]
                moved = strip if shift == 0 else pltpu.roll(strip, shift, 1)
                joined = moved if joined is None else jnp.where(lane == x, moved, joined)
            hist.append(joined)
    high, low = split(jnp.concatenate(hist, axis=0))
    spectrum = spectrum_ref[...].astype(jnp.bfloat16)
    modes = dot(high, spectrum[:TP]) + dot(low, spectrum[:TP]) + dot(high, spectrum[TP:])
    position = rest(lax.broadcasted_iota(jnp.int32, (2 * NBLK, tiles), 0), NBLK) == place_ref[...]
    position = jnp.where(position, 1.0, 0.0).T.astype(jnp.bfloat16)
    turns = dot(position, turns_ref[...].astype(jnp.bfloat16))
    cosine, sine = turns[:, :M], turns[:, M:]
    turned = []
    for c in range(CYCLE_DEV):
        real = modes[c * tiles : (c + 1) * tiles, :M]
        imag = modes[c * tiles : (c + 1) * tiles, M:]
        turned += [real * cosine - imag * sine, real * sine + imag * cosine]
    bins = SHELL_DEV * owners
    key = shell_ref[...] * owners + block_ref[...]
    hot = lax.broadcasted_iota(jnp.int32, (bins, tiles), 0) == key
    hot = jnp.where(hot, 1.0, 0.0).astype(jnp.bfloat16)
    high, low = split(jnp.concatenate(turned, axis=1))
    binned = dot(hot, high) + dot(hot, low)
    pieces = [binned[:, n * M : (n + 1) * M] for n in range(2 * CYCLE_DEV)]
    near = math.exp(-0.5)
    pieces = [
        pieces[2 * k + part] + near * pieces[2 * (1 - k) + part]
        for k in range(CYCLE_DEV)
        for part in range(2)
    ]
    share = M // sky_count
    width = len(pieces) * share
    lane = quotient(lax.broadcasted_iota(jnp.int32, (bins, M), 1), share)
    for z in range(sky_count):
        message = None
        for n, piece in enumerate(pieces):
            shift = (n - z) * share % M
            moved = piece if shift == 0 else pltpu.roll(piece, shift, 1)
            message = moved if message is None else jnp.where(lane == n, moved, message)
        out_ref[z] = message[:, :width]


def kernel(
    counts, per, blocks, cycles, cycle_hbm, pixel_hbm, mass_hbm, block_hbm, shell_hbm, place_hbm,
    spectrum_hbm, turns_hbm, weight_hbm, basis_ref, out_ref,
    cycle_ref, pixel_ref, mass_ref, block_ref, shell_ref, place_ref, spectrum_ref, turns_ref,
    weight_ref, key_ref, fine_ref, high_ref, low_ref, hist_ref, parts_ref,
    halves, arrived, fetch_sem, own_sem, half_send, half_recv, part_send, part_recv,
):
    fetches = [
        pltpu.make_async_copy(source, target, fetch_sem.at[n])
        for n, (source, target) in enumerate(
            (
                *(
                    (array.at[:, h * SIDE : (h + 1) * SIDE], held.at[h])
                    for array, held in (
                        (cycle_hbm, cycle_ref),
                        (pixel_hbm, pixel_ref),
                        (mass_hbm, mass_ref),
                    )
                    for h in range(cycle_ref.shape[0])
                ),
                (spectrum_hbm, spectrum_ref),
                (turns_hbm, turns_ref),
                (block_hbm, block_ref),
                (shell_hbm, shell_ref),
                (place_hbm, place_ref),
                (weight_hbm, weight_ref),
            )
        )
    ]
    for fetch in fetches:
        fetch.start()
    shell_count, sky_count, sub_count = counts
    shell, sky, sub = lax.axis_index("shell"), lax.axis_index("sky"), lax.axis_index("sub")
    peers = shell_count * sky_count * sub_count
    me = (shell * sky_count + sky) * sub_count + sub
    degrees = halves.shape[2]
    orders = basis_ref.shape[0] // cycles

    def place(rank):
        return dict(
            shell=quotient(rank, sky_count * sub_count),
            sky=rest(quotient(rank, sub_count), sky_count),
            sub=rest(rank, sub_count),
        )

    barrier = pltpu.get_barrier_semaphore()

    @pl.loop(1, peers, unroll=peers <= 16)
    def _(j):
        pl.semaphore_signal(
            barrier, inc=1, device_id=place(rest(me + j, peers)), device_id_type=MESH
        )

    def send(j):
        target = place(rest(me + j, peers))
        return pltpu.make_async_remote_copy(
            src_ref=parts_ref.at[target["sky"]],
            dst_ref=arrived.at[me],
            send_sem=part_send.at[j],
            recv_sem=part_recv.at[j],
            device_id=target,
            device_id_type=MESH,
        )

    def expect(j):
        source = rest(me + peers - j, peers)
        return pltpu.make_async_remote_copy(
            src_ref=parts_ref.at[0],
            dst_ref=arrived.at[source],
            send_sem=part_send.at[j],
            recv_sem=part_recv.at[j],
            device_id=place(source),
            device_id_type=MESH,
        )

    def half(j):
        target = rest(sub + j, sub_count)
        return pltpu.make_async_remote_copy(
            src_ref=basis_ref.at[:, pl.ds(pl.multiple_of(target * degrees, degrees), degrees)],
            dst_ref=halves.at[sub],
            send_sem=half_send.at[j],
            recv_sem=half_recv.at[j],
            device_id={"sub": target},
            device_id_type=MESH,
        )

    def expect_half(j):
        source = rest(sub + sub_count - j, sub_count)
        return pltpu.make_async_remote_copy(
            src_ref=basis_ref.at[:, pl.ds(0, degrees)],
            dst_ref=halves.at[source],
            send_sem=half_send.at[j],
            recv_sem=half_recv.at[j],
            device_id={"sub": source},
            device_id_type=MESH,
        )

    own = pltpu.make_async_copy(
        basis_ref.at[:, pl.ds(pl.multiple_of(sub * degrees, degrees), degrees)],
        halves.at[sub],
        own_sem,
    )
    own.start()

    def fetch_particles():
        for fetch in fetches[:-6]:
            fetch.wait()

    def fetch_tables():
        for fetch in fetches[-6:]:
            fetch.wait()

    def early():
        pl.semaphore_wait(barrier, peers - 1)
        for j in range(1, sub_count):
            half(j).start()

    deposit(
        sky_count, blocks, cycle_ref, pixel_ref, mass_ref, block_ref, shell_ref, place_ref,
        spectrum_ref, turns_ref, parts_ref, key_ref, fine_ref, high_ref, low_ref, hist_ref,
        fetch_particles, fetch_tables, early,
    )

    @pl.loop(1, peers, unroll=peers <= 16)
    def _(j):
        send(j).start()

    arrived[me] = parts_ref[sky]

    @pl.loop(1, peers, unroll=peers <= 16)
    def _(j):
        expect(j).wait_recv()

    group = sky_count * sub_count
    folded = [None] * per
    for x in range(shell_count):
        total = jnp.sum(arrived[x * group : (x + 1) * group], axis=0)
        modes = (total * (2.0 * math.pi / NP)).astype(jnp.bfloat16).astype(jnp.float32)
        for s in range(SHELL_DEV):
            part = modes[s * blocks : (s + 1) * blocks]
            lens = x * SHELL_DEV + s
            for i in range(per):
                source = shell * per + i
                weight = jnp.where(lens <= source, weight_ref[source, lens], 0.0)
                term = weight * part
                folded[i] = term if folded[i] is None else folded[i] + term
    folded = jnp.concatenate(split(jnp.concatenate(folded, axis=0)), axis=0)
    width = folded.shape[1]
    to = lax.broadcasted_iota(jnp.int32, (width, width), 0)
    within = rest(to, 2 * orders)
    source = to - within + rest(to, 2) * orders + quotient(within, 2)
    swap = source == lax.broadcasted_iota(jnp.int32, (width, width), 1)
    swap = jnp.where(swap, 1.0, 0.0).astype(jnp.bfloat16)
    coefficients = dot(swap, folded, 1).astype(jnp.bfloat16)
    depth = orders * cycles
    span = 2 * orders
    lane = lax.broadcasted_iota(jnp.int32, (2 * per * blocks, depth), 1)
    row = lax.broadcasted_iota(jnp.int32, (2 * per * blocks, depth), 0)
    lane_out = lax.broadcasted_iota(jnp.int32, (span, depth), 1)
    diagonal = quotient(lane_out, cycles) == quotient(
        lax.broadcasted_iota(jnp.int32, (span, depth), 0), 2
    )
    even = rest(lane_out, CYCLE_DEV) == 0
    turn = quotient(rest(lane, cycles), CYCLE_DEV)
    left = []
    for h in range(sub_count):
        rows = []
        for piece in range(2):
            for i in range(per):
                block = (piece * per + i) * blocks + h * (cycles // CYCLE_DEV) + turn
                pick = jnp.where(row == block, 1.0, 0.0).astype(jnp.bfloat16)
                spread = dot(coefficients, pick)
                chosen = jnp.where(even, spread[:span], spread[span:])
                rows.append(jnp.where(diagonal, chosen, 0.0).astype(jnp.bfloat16))
        left.append(jnp.concatenate(rows, axis=0))
    own.wait()
    for j in range(1, sub_count):
        expect_half(j).wait_recv()
    step = 256

    @pl.loop(0, degrees // step)
    def _(n):
        columns = pl.ds(pl.multiple_of(n * step, step), step)
        result = None
        for h in range(sub_count):
            term = dot(left[h], halves[h, :, columns])
            result = term if result is None else result + term
        result = result[: per * span] + result[per * span :]
        for i in range(per):
            out_ref[i, :, :, columns] = result[i * span : (i + 1) * span].reshape(orders, 2, step)

    for j in range(1, sub_count):
        half(j).wait_send()

    @pl.loop(1, peers, unroll=peers <= 16)
    def _(j):
        send(j).wait_send()


def body(
    part_cycle,
    part_pixel,
    part_mass,
    tile_block,
    tile_shell,
    tile_pixel,
    harmonic_basis,
    lens_weight,
):
    shell_count, sky_count, sub_count = (
        lax.axis_size("shell"),
        lax.axis_size("sky"),
        lax.axis_size("sub"),
    )
    owners = sky_count * sub_count
    peers = shell_count * owners
    tiles, particles = part_cycle.shape[1:]
    orders, cycles, degrees = harmonic_basis.shape
    per = lens_weight.shape[0] // shell_count
    share = degrees // sub_count
    bins = SHELL_DEV * owners
    width = 2 * CYCLE_DEV * orders
    spectrum, turns = tables()
    result = pl.pallas_call(
        functools.partial(kernel, (shell_count, sky_count, sub_count), per, owners, cycles),
        out_shape=pltpu.VMEM((per, orders, 2, share), jnp.float32),
        in_specs=[pl.BlockSpec(memory_space=pltpu.HBM)] * 10,
        out_specs=pl.BlockSpec(memory_space=pltpu.VMEM),
        scratch_shapes=[
            pltpu.VMEM((particles // SIDE, tiles, SIDE), jnp.int32),
            pltpu.VMEM((particles // SIDE, tiles, SIDE), jnp.int32),
            pltpu.VMEM((particles // SIDE, tiles, SIDE), jnp.float32),
            pltpu.VMEM((1, tiles), jnp.int32),
            pltpu.VMEM((1, tiles), jnp.int32),
            pltpu.VMEM((1, tiles), jnp.int32),
            pltpu.VMEM(spectrum.shape, jnp.float32),
            pltpu.VMEM(turns.shape, jnp.float32),
            pltpu.SMEM(lens_weight.shape, jnp.float32),
            pltpu.VMEM((particles // SIDE, tiles, SIDE), jnp.int32),
            pltpu.VMEM((particles // SIDE, tiles, SIDE), jnp.float32),
            pltpu.VMEM((particles // SIDE, tiles, SIDE), jnp.float32),
            pltpu.VMEM((particles // SIDE, tiles, SIDE), jnp.float32),
            pltpu.VMEM((2, tiles * CYCLE_DEV * TP // (2 * SIDE), SIDE), jnp.float32),
            pltpu.VMEM((sky_count, bins, width), jnp.float32),
            pltpu.VMEM((sub_count, orders * cycles, share), jnp.bfloat16),
            pltpu.VMEM((peers, bins, width), jnp.float32),
            pltpu.SemaphoreType.DMA((3 * (particles // SIDE) + 6,)),
            pltpu.SemaphoreType.DMA,
            pltpu.SemaphoreType.DMA((sub_count,)),
            pltpu.SemaphoreType.DMA((sub_count,)),
            pltpu.SemaphoreType.DMA((peers,)),
            pltpu.SemaphoreType.DMA((peers,)),
        ],
        compiler_params=pltpu.CompilerParams(
            collective_id=0, has_side_effects=True, vmem_limit_bytes=60 << 20
        ),
        name="modes",
    )(
        part_cycle[0],
        part_pixel[0],
        part_mass[0],
        tile_block.reshape(1, tiles),
        tile_shell,
        tile_pixel,
        spectrum,
        turns,
        lens_weight,
        harmonic_basis.reshape(orders * cycles, degrees),
    )
    return result


def solution(mesh):
    return jax.shard_map(
        body,
        mesh=mesh,
        in_specs=(
            P("shell", ("sky", "sub"), None),
            P("shell", ("sky", "sub"), None),
            P("shell", ("sky", "sub"), None),
            P("shell", ("sky", "sub"), None),
            P("shell", ("sky", "sub")),
            P("shell", ("sky", "sub")),
            P("sky", "sub", None),
            P(),
        ),
        out_specs=P(("groups", "shell"), "sky", None, "sub"),
        check_vma=False,
    )
```

```python
import functools
import math

import jax
import jax.numpy as jnp
import numpy as np
from jax import lax
from jax.experimental import pallas as pl
from jax.experimental.pallas import tpu as pltpu
from jax.sharding import PartitionSpec as P

NP = 8192
M = 128
TP = 128
CYCLE_DEV = 2
SHELL_DEV = 2
NBLK = NP // TP

MESH = pl.DeviceIdType.MESH


def tables():
    pixel = np.arange(TP, dtype=np.float64)
    smooth = np.exp(-((pixel[:, None] - pixel[None, :]) ** 2) / 18.0)
    orders = np.arange(M)
    angle = 2.0 * math.pi * ((np.arange(TP)[:, None] * orders[None, :]) % NP) / NP
    turn = 2.0 * math.pi * ((np.arange(NBLK)[:, None] * TP * orders[None, :]) % NP) / NP
    spectrum = np.concatenate([smooth @ np.cos(angle), -(smooth @ np.sin(angle))], axis=1)
    turns = np.concatenate([np.cos(turn), -np.sin(turn)], axis=1)

    def split(table):
        high = table.astype(jnp.bfloat16)
        low = (table - high.astype(np.float64)).astype(jnp.bfloat16)
        return np.concatenate([high, low], axis=0).astype(np.float32)

    return split(spectrum), split(turns)


def split(values):
    high = values.astype(jnp.bfloat16)
    return high, (values - high.astype(jnp.float32)).astype(jnp.bfloat16)


def dot(one, two, right=0):
    return lax.dot_general(
        one, two, (((1,), (right,)), ((), ())), preferred_element_type=jnp.float32
    )


FINE = 32
SIDE = 128


def quotient(value, by):
    return value >> (by.bit_length() - 1) if by & (by - 1) == 0 else value // by


def rest(value, by):
    return value & (by - 1) if by & (by - 1) == 0 else value % by


def deposit(
    sky_count, owners, cycle_ref, pixel_ref, mass_ref, block_ref, shell_ref, place_ref, spectrum_ref,
    turns_ref, out_ref, key_ref, fine_ref, high_ref, low_ref, hist_ref, fetch_particles, fetch_tables,
    early,
):
    halves, tiles = pixel_ref.shape[:2]
    coarse = TP // FINE
    bundle = 2 * SIDE // FINE
    groups = tiles // bundle
    keys = CYCLE_DEV * coarse
    fetch_particles()
    masses = mass_ref[...]
    pixels = pixel_ref[...]
    high = masses.astype(jnp.bfloat16).astype(jnp.float32)
    high_ref[...] = high
    low_ref[...] = masses - high
    fine_ref[...] = rest(pixels, FINE).astype(jnp.float32)
    key_ref[...] = cycle_ref[...] * coarse + quotient(pixels, FINE)
    fine_ids = lax.broadcasted_iota(jnp.int32, (FINE, SIDE), 0)
    fine_ids = fine_ids.astype(jnp.float32).astype(jnp.bfloat16)
    ones, zeros = jnp.ones((FINE, SIDE), jnp.bfloat16), jnp.zeros((FINE, SIDE), jnp.bfloat16)
    key_ids = lax.broadcasted_iota(jnp.int32, (keys, SIDE), 0)
    same = (
        quotient(lax.broadcasted_iota(jnp.int32, (bundle * keys, bundle * FINE), 0), keys)
        == quotient(lax.broadcasted_iota(jnp.int32, (bundle * keys, bundle * FINE), 1), FINE)
    )

    def group(g, carry):
        spread, highs, lows = [], [], []
        for t in range(bundle):
            row = pl.ds(t * groups + g, 1)
            spread_t, high_t, low_t = [], [], []
            for h in range(halves):
                fine = jnp.broadcast_to(fine_ref[h, row, :], (FINE, SIDE)).astype(jnp.bfloat16)
                spread_t.append(jnp.where(fine == fine_ids, ones, zeros))
                here = jnp.broadcast_to(key_ref[h, row, :], (keys, SIDE)) == key_ids
                high_t.append(
                    jnp.where(here, jnp.broadcast_to(high_ref[h, row, :], (keys, SIDE)), 0.0)
                )
                low_t.append(
                    jnp.where(here, jnp.broadcast_to(low_ref[h, row, :], (keys, SIDE)), 0.0)
                )
            spread.append(jnp.concatenate(spread_t, axis=1))
            highs.append(jnp.concatenate(high_t, axis=1))
            lows.append(jnp.concatenate(low_t, axis=1))
        weights = jnp.concatenate(highs + lows, axis=0).astype(jnp.bfloat16)
        pairs = dot(weights, jnp.concatenate(spread, axis=0), 1)
        count = bundle * keys
        pairs = jnp.where(same, pairs[:count] + pairs[count:], 0.0)
        own = jnp.sum(pairs.reshape(bundle, keys, bundle * FINE), axis=0)
        at = pl.ds(pl.multiple_of(g * keys, keys), keys)
        for side in range(bundle * FINE // SIDE):
            hist_ref[side, at, :] = own[:, side * SIDE : (side + 1) * SIDE]
        return carry

    lax.fori_loop(0, groups // 2, group, 0, unroll=16)
    early()
    lax.fori_loop(groups // 2, groups, group, 0, unroll=16)
    fetch_tables()
    lane = quotient(lax.broadcasted_iota(jnp.int32, (groups, SIDE), 1), FINE)
    strips = [
        [hist_ref[side, pl.ds(key, groups, stride=keys), :] for key in range(keys)]
        for side in range(bundle * FINE // SIDE)
    ]
    hist = []
    for c in range(CYCLE_DEV):
        for t in range(bundle):
            side, offset = t * FINE // SIDE, t * FINE % SIDE
            joined = None
            for x in range(coarse):
                shift = (x * FINE - offset) % SIDE
                strip = strips[side][c * coarse + x]
                moved = strip if shift == 0 else pltpu.roll(strip, shift, 1)
                joined = moved if joined is None else jnp.where(lane == x, moved, joined)
            hist.append(joined)
    high, low = split(jnp.concatenate(hist, axis=0))
    spectrum = spectrum_ref[...].astype(jnp.bfloat16)
    modes = dot(high, spectrum[:TP]) + dot(low, spectrum[:TP]) + dot(high, spectrum[TP:])
    position = rest(lax.broadcasted_iota(jnp.int32, (2 * NBLK, tiles), 0), NBLK) == place_ref[...]
    position = jnp.where(position, 1.0, 0.0).T.astype(jnp.bfloat16)
    turns = dot(position, turns_ref[...].astype(jnp.bfloat16))
    cosine, sine = turns[:, :M], turns[:, M:]
    turned = []
    for c in range(CYCLE_DEV):
        real = modes[c * tiles : (c + 1) * tiles, :M]
        imag = modes[c * tiles : (c + 1) * tiles, M:]
        turned += [real * cosine - imag * sine, real * sine + imag * cosine]
    bins = SHELL_DEV * owners
    key = shell_ref[...] * owners + block_ref[...]
    hot = lax.broadcasted_iota(jnp.int32, (bins, tiles), 0) == key
    hot = jnp.where(hot, 1.0, 0.0).astype(jnp.bfloat16)
    high, low = split(jnp.concatenate(turned, axis=1))
    binned = dot(hot, high) + dot(hot, low)
    pieces = [binned[:, n * M : (n + 1) * M] for n in range(2 * CYCLE_DEV)]
    near = math.exp(-0.5)
    pieces = [
        pieces[2 * k + part] + near * pieces[2 * (1 - k) + part]
        for k in range(CYCLE_DEV)
        for part in range(2)
    ]
    share = M // sky_count
    width = len(pieces) * share
    lane = quotient(lax.broadcasted_iota(jnp.int32, (bins, M), 1), share)
    for z in range(sky_count):
        message = None
        for n, piece in enumerate(pieces):
            shift = (n - z) * share % M
            moved = piece if shift == 0 else pltpu.roll(piece, shift, 1)
            message = moved if message is None else jnp.where(lane == n, moved, message)
        out_ref[z] = message[:, :width]


def kernel(
    counts, per, blocks, cycles, cycle_hbm, pixel_hbm, mass_hbm, block_hbm, shell_hbm, place_hbm,
    spectrum_hbm, turns_hbm, weight_hbm, basis_ref, out_ref,
    cycle_ref, pixel_ref, mass_ref, block_ref, shell_ref, place_ref, spectrum_ref, turns_ref,
    weight_ref, key_ref, fine_ref, high_ref, low_ref, hist_ref, parts_ref,
    halves, arrived, fetch_sem, own_sem, half_send, half_recv, part_send, part_recv,
):
    fetches = [
        pltpu.make_async_copy(source, target, fetch_sem.at[n])
        for n, (source, target) in enumerate(
            (
                *(
                    (array.at[:, h * SIDE : (h + 1) * SIDE], held.at[h])
                    for array, held in (
                        (cycle_hbm, cycle_ref),
                        (pixel_hbm, pixel_ref),
                        (mass_hbm, mass_ref),
                    )
                    for h in range(cycle_ref.shape[0])
                ),
                (spectrum_hbm, spectrum_ref),
                (turns_hbm, turns_ref),
                (block_hbm, block_ref),
                (shell_hbm, shell_ref),
                (place_hbm, place_ref),
                (weight_hbm, weight_ref),
            )
        )
    ]
    for fetch in fetches:
        fetch.start()
    shell_count, sky_count, sub_count = counts
    shell, sky, sub = lax.axis_index("shell"), lax.axis_index("sky"), lax.axis_index("sub")
    peers = shell_count * sky_count * sub_count
    me = (shell * sky_count + sky) * sub_count + sub
    degrees = halves.shape[2]
    orders = basis_ref.shape[0] // cycles

    def place(rank):
        return dict(
            shell=quotient(rank, sky_count * sub_count),
            sky=rest(quotient(rank, sub_count), sky_count),
            sub=rest(rank, sub_count),
        )

    barrier = pltpu.get_barrier_semaphore()

    @pl.loop(1, peers, unroll=peers <= 16)
    def _(j):
        pl.semaphore_signal(
            barrier, inc=1, device_id=place(rest(me + j, peers)), device_id_type=MESH
        )

    def send(j):
        target = place(rest(me + j, peers))
        return pltpu.make_async_remote_copy(
            src_ref=parts_ref.at[target["sky"]],
            dst_ref=arrived.at[me],
            send_sem=part_send.at[j],
            recv_sem=part_recv.at[j],
            device_id=target,
            device_id_type=MESH,
        )

    def expect(j):
        source = rest(me + peers - j, peers)
        return pltpu.make_async_remote_copy(
            src_ref=parts_ref.at[0],
            dst_ref=arrived.at[source],
            send_sem=part_send.at[j],
            recv_sem=part_recv.at[j],
            device_id=place(source),
            device_id_type=MESH,
        )

    def half(j):
        target = rest(sub + j, sub_count)
        return pltpu.make_async_remote_copy(
            src_ref=basis_ref.at[:, pl.ds(pl.multiple_of(target * degrees, degrees), degrees)],
            dst_ref=halves.at[sub],
            send_sem=half_send.at[j],
            recv_sem=half_recv.at[j],
            device_id={"sub": target},
            device_id_type=MESH,
        )

    def expect_half(j):
        source = rest(sub + sub_count - j, sub_count)
        return pltpu.make_async_remote_copy(
            src_ref=basis_ref.at[:, pl.ds(0, degrees)],
            dst_ref=halves.at[source],
            send_sem=half_send.at[j],
            recv_sem=half_recv.at[j],
            device_id={"sub": source},
            device_id_type=MESH,
        )

    own = pltpu.make_async_copy(
        basis_ref.at[:, pl.ds(pl.multiple_of(sub * degrees, degrees), degrees)],
        halves.at[sub],
        own_sem,
    )
    own.start()

    def fetch_particles():
        for fetch in fetches[:-6]:
            fetch.wait()

    def fetch_tables():
        for fetch in fetches[-6:]:
            fetch.wait()

    def early():
        pl.semaphore_wait(barrier, peers - 1)
        for j in range(1, sub_count):
            half(j).start()

    deposit(
        sky_count, blocks, cycle_ref, pixel_ref, mass_ref, block_ref, shell_ref, place_ref,
        spectrum_ref, turns_ref, parts_ref, key_ref, fine_ref, high_ref, low_ref, hist_ref,
        fetch_particles, fetch_tables, early,
    )

    @pl.loop(1, peers, unroll=peers <= 16)
    def _(j):
        send(j).start()

    arrived[me] = parts_ref[sky]

    @pl.loop(1, peers, unroll=peers <= 16)
    def _(j):
        expect(j).wait_recv()

    group = sky_count * sub_count
    folded = [None] * per
    for x in range(shell_count):
        total = jnp.sum(arrived[x * group : (x + 1) * group], axis=0)
        modes = (total * (2.0 * math.pi / NP)).astype(jnp.bfloat16).astype(jnp.float32)
        for s in range(SHELL_DEV):
            part = modes[s * blocks : (s + 1) * blocks]
            lens = x * SHELL_DEV + s
            for i in range(per):
                source = shell * per + i
                weight = jnp.where(lens <= source, weight_ref[source, lens], 0.0)
                term = weight * part
                folded[i] = term if folded[i] is None else folded[i] + term
    folded = jnp.concatenate(split(jnp.concatenate(folded, axis=0)), axis=0)
    width = folded.shape[1]
    to = lax.broadcasted_iota(jnp.int32, (width, width), 0)
    within = rest(to, 2 * orders)
    source = to - within + rest(to, 2) * orders + quotient(within, 2)
    swap = source == lax.broadcasted_iota(jnp.int32, (width, width), 1)
    swap = jnp.where(swap, 1.0, 0.0).astype(jnp.bfloat16)
    coefficients = dot(swap, folded, 1).astype(jnp.bfloat16)
    depth = orders * cycles
    span = 2 * orders
    lane = lax.broadcasted_iota(jnp.int32, (2 * per * blocks, depth), 1)
    row = lax.broadcasted_iota(jnp.int32, (2 * per * blocks, depth), 0)
    lane_out = lax.broadcasted_iota(jnp.int32, (span, depth), 1)
    diagonal = quotient(lane_out, cycles) == quotient(
        lax.broadcasted_iota(jnp.int32, (span, depth), 0), 2
    )
    even = rest(lane_out, CYCLE_DEV) == 0
    turn = quotient(rest(lane, cycles), CYCLE_DEV)
    left = []
    for h in range(sub_count):
        rows = []
        for piece in range(2):
            for i in range(per):
                block = (piece * per + i) * blocks + h * (cycles // CYCLE_DEV) + turn
                pick = jnp.where(row == block, 1.0, 0.0).astype(jnp.bfloat16)
                spread = dot(coefficients, pick)
                chosen = jnp.where(even, spread[:span], spread[span:])
                rows.append(jnp.where(diagonal, chosen, 0.0).astype(jnp.bfloat16))
        left.append(jnp.concatenate(rows, axis=0))
    own.wait()
    for j in range(1, sub_count):
        expect_half(j).wait_recv()
    step = 512
    for first in range(0, degrees, step):
        columns = slice(first, first + step)
        result = None
        for h in range(sub_count):
            term = jnp.dot(left[h], halves[h, :, columns], preferred_element_type=jnp.float32)
            result = term if result is None else result + term
        result = result[: per * span] + result[per * span :]
        for i in range(per):
            out_ref[i, :, :, columns] = result[i * span : (i + 1) * span].reshape(orders, 2, step)
    for j in range(1, sub_count):
        half(j).wait_send()

    @pl.loop(1, peers, unroll=peers <= 16)
    def _(j):
        send(j).wait_send()


def body(
    part_cycle,
    part_pixel,
    part_mass,
    tile_block,
    tile_shell,
    tile_pixel,
    harmonic_basis,
    lens_weight,
):
    shell_count, sky_count, sub_count = (
        lax.axis_size("shell"),
        lax.axis_size("sky"),
        lax.axis_size("sub"),
    )
    owners = sky_count * sub_count
    peers = shell_count * owners
    tiles, particles = part_cycle.shape[1:]
    orders, cycles, degrees = harmonic_basis.shape
    per = lens_weight.shape[0] // shell_count
    share = degrees // sub_count
    bins = SHELL_DEV * owners
    width = 2 * CYCLE_DEV * orders
    spectrum, turns = tables()
    result = pl.pallas_call(
        functools.partial(kernel, (shell_count, sky_count, sub_count), per, owners, cycles),
        out_shape=pltpu.VMEM((per, orders, 2, share), jnp.float32),
        in_specs=[pl.BlockSpec(memory_space=pltpu.HBM)] * 10,
        out_specs=pl.BlockSpec(memory_space=pltpu.VMEM),
        scratch_shapes=[
            pltpu.VMEM((particles // SIDE, tiles, SIDE), jnp.int32),
            pltpu.VMEM((particles // SIDE, tiles, SIDE), jnp.int32),
            pltpu.VMEM((particles // SIDE, tiles, SIDE), jnp.float32),
            pltpu.VMEM((1, tiles), jnp.int32),
            pltpu.VMEM((1, tiles), jnp.int32),
            pltpu.VMEM((1, tiles), jnp.int32),
            pltpu.VMEM(spectrum.shape, jnp.float32),
            pltpu.VMEM(turns.shape, jnp.float32),
            pltpu.SMEM(lens_weight.shape, jnp.float32),
            pltpu.VMEM((particles // SIDE, tiles, SIDE), jnp.int32),
            pltpu.VMEM((particles // SIDE, tiles, SIDE), jnp.float32),
            pltpu.VMEM((particles // SIDE, tiles, SIDE), jnp.float32),
            pltpu.VMEM((particles // SIDE, tiles, SIDE), jnp.float32),
            pltpu.VMEM((2, tiles * CYCLE_DEV * TP // (2 * SIDE), SIDE), jnp.float32),
            pltpu.VMEM((sky_count, bins, width), jnp.float32),
            pltpu.VMEM((sub_count, orders * cycles, share), jnp.bfloat16),
            pltpu.VMEM((peers, bins, width), jnp.float32),
            pltpu.SemaphoreType.DMA((3 * (particles // SIDE) + 6,)),
            pltpu.SemaphoreType.DMA,
            pltpu.SemaphoreType.DMA((sub_count,)),
            pltpu.SemaphoreType.DMA((sub_count,)),
            pltpu.SemaphoreType.DMA((peers,)),
            pltpu.SemaphoreType.DMA((peers,)),
        ],
        compiler_params=pltpu.CompilerParams(
            collective_id=0, has_side_effects=True, vmem_limit_bytes=60 << 20
        ),
        name="modes",
    )(
        part_cycle[0],
        part_pixel[0],
        part_mass[0],
        tile_block.reshape(1, tiles),
        tile_shell,
        tile_pixel,
        spectrum,
        turns,
        lens_weight,
        harmonic_basis.reshape(orders * cycles, degrees),
    )
    return result


def solution(mesh):
    return jax.shard_map(
        body,
        mesh=mesh,
        in_specs=(
            P("shell", ("sky", "sub"), None),
            P("shell", ("sky", "sub"), None),
            P("shell", ("sky", "sub"), None),
            P("shell", ("sky", "sub"), None),
            P("shell", ("sky", "sub")),
            P("shell", ("sky", "sub")),
            P("sky", "sub", None),
            P(),
        ),
        out_specs=P(("groups", "shell"), "sky", None, "sub"),
        check_vma=False,
    )
```

```python
import functools
import math

import jax
import jax.numpy as jnp
import numpy as np
from jax import lax
from jax.experimental import pallas as pl
from jax.experimental.pallas import tpu as pltpu
from jax.sharding import PartitionSpec as P

NP = 8192
M = 128
TP = 128
CYCLE_DEV = 2
SHELL_DEV = 2
NBLK = NP // TP

MESH = pl.DeviceIdType.MESH


def tables():
    pixel = np.arange(TP, dtype=np.float64)
    smooth = np.exp(-((pixel[:, None] - pixel[None, :]) ** 2) / 18.0)
    orders = np.arange(M)
    angle = 2.0 * math.pi * ((np.arange(TP)[:, None] * orders[None, :]) % NP) / NP
    turn = 2.0 * math.pi * ((np.arange(NBLK)[:, None] * TP * orders[None, :]) % NP) / NP
    spectrum = np.concatenate([smooth @ np.cos(angle), -(smooth @ np.sin(angle))], axis=1)
    turns = np.concatenate([np.cos(turn), -np.sin(turn)], axis=1)

    def split(table):
        high = table.astype(jnp.bfloat16)
        low = (table - high.astype(np.float64)).astype(jnp.bfloat16)
        return np.concatenate([high, low], axis=0).astype(np.float32)

    return split(spectrum), split(turns)


def split(values):
    high = values.astype(jnp.bfloat16)
    return high, (values - high.astype(jnp.float32)).astype(jnp.bfloat16)


def dot(one, two, right=0):
    return lax.dot_general(
        one, two, (((1,), (right,)), ((), ())), preferred_element_type=jnp.float32
    )


FINE = 32
SIDE = 128


def quotient(value, by):
    return value >> (by.bit_length() - 1) if by & (by - 1) == 0 else value // by


def rest(value, by):
    return value & (by - 1) if by & (by - 1) == 0 else value % by


def deposit(
    sky_count, owners, cycle_ref, pixel_ref, mass_ref, block_ref, shell_ref, place_ref, spectrum_ref,
    turns_ref, out_ref, key_ref, fine_ref, high_ref, low_ref, hist_ref, fetch_particles, fetch_tables,
    early,
):
    halves, tiles = pixel_ref.shape[:2]
    coarse = TP // FINE
    bundle = 2 * SIDE // FINE
    groups = tiles // bundle
    keys = CYCLE_DEV * coarse
    fetch_particles()
    masses = mass_ref[...]
    pixels = pixel_ref[...]
    high = masses.astype(jnp.bfloat16).astype(jnp.float32)
    high_ref[...] = high
    low_ref[...] = masses - high
    fine_ref[...] = rest(pixels, FINE).astype(jnp.float32)
    key_ref[...] = cycle_ref[...] * coarse + quotient(pixels, FINE)
    fine_ids = lax.broadcasted_iota(jnp.int32, (FINE, SIDE), 0)
    fine_ids = fine_ids.astype(jnp.float32).astype(jnp.bfloat16)
    ones, zeros = jnp.ones((FINE, SIDE), jnp.bfloat16), jnp.zeros((FINE, SIDE), jnp.bfloat16)
    key_ids = lax.broadcasted_iota(jnp.int32, (keys, SIDE), 0)
    same = (
        quotient(lax.broadcasted_iota(jnp.int32, (bundle * keys, bundle * FINE), 0), keys)
        == quotient(lax.broadcasted_iota(jnp.int32, (bundle * keys, bundle * FINE), 1), FINE)
    )

    def group(g, carry):
        spread, highs, lows = [], [], []
        for t in range(bundle):
            row = pl.ds(t * groups + g, 1)
            spread_t, high_t, low_t = [], [], []
            for h in range(halves):
                fine = jnp.broadcast_to(fine_ref[h, row, :], (FINE, SIDE)).astype(jnp.bfloat16)
                spread_t.append(jnp.where(fine == fine_ids, ones, zeros))
                here = jnp.broadcast_to(key_ref[h, row, :], (keys, SIDE)) == key_ids
                high_t.append(
                    jnp.where(here, jnp.broadcast_to(high_ref[h, row, :], (keys, SIDE)), 0.0)
                )
                low_t.append(
                    jnp.where(here, jnp.broadcast_to(low_ref[h, row, :], (keys, SIDE)), 0.0)
                )
            spread.append(jnp.concatenate(spread_t, axis=1))
            highs.append(jnp.concatenate(high_t, axis=1))
            lows.append(jnp.concatenate(low_t, axis=1))
        weights = jnp.concatenate(highs + lows, axis=0).astype(jnp.bfloat16)
        pairs = dot(weights, jnp.concatenate(spread, axis=0), 1)
        count = bundle * keys
        pairs = jnp.where(same, pairs[:count] + pairs[count:], 0.0)
        own = jnp.sum(pairs.reshape(bundle, keys, bundle * FINE), axis=0)
        at = pl.ds(pl.multiple_of(g * keys, keys), keys)
        for side in range(bundle * FINE // SIDE):
            hist_ref[side, at, :] = own[:, side * SIDE : (side + 1) * SIDE]
        return carry

    lax.fori_loop(0, groups, group, 0, unroll=32)
    early()
    fetch_tables()
    lane = quotient(lax.broadcasted_iota(jnp.int32, (groups, SIDE), 1), FINE)
    strips = [
        [hist_ref[side, pl.ds(key, groups, stride=keys), :] for key in range(keys)]
        for side in range(bundle * FINE // SIDE)
    ]
    hist = []
    for c in range(CYCLE_DEV):
        for t in range(bundle):
            side, offset = t * FINE // SIDE, t * FINE % SIDE
            joined = None
            for x in range(coarse):
                shift = (x * FINE - offset) % SIDE
                strip = strips[side][c * coarse + x]
                moved = strip if shift == 0 else pltpu.roll(strip, shift, 1)
                joined = moved if joined is None else jnp.where(lane == x, moved, joined)
            hist.append(joined)
    high, low = split(jnp.concatenate(hist, axis=0))
    spectrum = spectrum_ref[...].astype(jnp.bfloat16)
    modes = dot(high, spectrum[:TP]) + dot(low, spectrum[:TP]) + dot(high, spectrum[TP:])
    position = rest(lax.broadcasted_iota(jnp.int32, (2 * NBLK, tiles), 0), NBLK) == place_ref[...]
    position = jnp.where(position, 1.0, 0.0).T.astype(jnp.bfloat16)
    turns = dot(position, turns_ref[...].astype(jnp.bfloat16))
    cosine, sine = turns[:, :M], turns[:, M:]
    turned = []
    for c in range(CYCLE_DEV):
        real = modes[c * tiles : (c + 1) * tiles, :M]
        imag = modes[c * tiles : (c + 1) * tiles, M:]
        turned += [real * cosine - imag * sine, real * sine + imag * cosine]
    bins = SHELL_DEV * owners
    key = shell_ref[...] * owners + block_ref[...]
    hot = lax.broadcasted_iota(jnp.int32, (bins, tiles), 0) == key
    hot = jnp.where(hot, 1.0, 0.0).astype(jnp.bfloat16)
    high, low = split(jnp.concatenate(turned, axis=1))
    binned = dot(hot, high) + dot(hot, low)
    pieces = [binned[:, n * M : (n + 1) * M] for n in range(2 * CYCLE_DEV)]
    near = math.exp(-0.5)
    pieces = [
        pieces[2 * k + part] + near * pieces[2 * (1 - k) + part]
        for k in range(CYCLE_DEV)
        for part in range(2)
    ]
    share = M // sky_count
    width = len(pieces) * share
    lane = quotient(lax.broadcasted_iota(jnp.int32, (bins, M), 1), share)
    for z in range(sky_count):
        message = None
        for n, piece in enumerate(pieces):
            shift = (n - z) * share % M
            moved = piece if shift == 0 else pltpu.roll(piece, shift, 1)
            message = moved if message is None else jnp.where(lane == n, moved, message)
        out_ref[z] = message[:, :width]


def kernel(
    counts, per, blocks, cycles, cycle_hbm, pixel_hbm, mass_hbm, block_hbm, shell_hbm, place_hbm,
    spectrum_hbm, turns_hbm, weight_hbm, basis_ref, out_ref,
    cycle_ref, pixel_ref, mass_ref, block_ref, shell_ref, place_ref, spectrum_ref, turns_ref,
    weight_ref, key_ref, fine_ref, high_ref, low_ref, hist_ref, parts_ref,
    halves, arrived, rounded, fetch_sem, own_sem, half_send, half_recv, part_send, part_recv,
    sum_send, sum_recv,
):
    fetches = [
        pltpu.make_async_copy(source, target, fetch_sem.at[n])
        for n, (source, target) in enumerate(
            (
                *(
                    (array.at[:, h * SIDE : (h + 1) * SIDE], held.at[h])
                    for array, held in (
                        (cycle_hbm, cycle_ref),
                        (pixel_hbm, pixel_ref),
                        (mass_hbm, mass_ref),
                    )
                    for h in range(cycle_ref.shape[0])
                ),
                (spectrum_hbm, spectrum_ref),
                (turns_hbm, turns_ref),
                (block_hbm, block_ref),
                (shell_hbm, shell_ref),
                (place_hbm, place_ref),
                (weight_hbm, weight_ref),
            )
        )
    ]
    for fetch in fetches:
        fetch.start()
    shell_count, sky_count, sub_count = counts
    shell, sky, sub = lax.axis_index("shell"), lax.axis_index("sky"), lax.axis_index("sub")
    peers = shell_count * sky_count * sub_count
    me = (shell * sky_count + sky) * sub_count + sub
    degrees = halves.shape[2]
    rows = arrived.shape[1]
    orders = basis_ref.shape[0] // cycles

    def place(rank):
        return dict(
            shell=quotient(rank, sky_count * sub_count),
            sky=rest(quotient(rank, sub_count), sky_count),
            sub=rest(rank, sub_count),
        )

    barrier = pltpu.get_barrier_semaphore()

    @pl.loop(1, peers, unroll=peers <= 16)
    def _(j):
        pl.semaphore_signal(
            barrier, inc=1, device_id=place(rest(me + j, peers)), device_id_type=MESH
        )

    def send(j):
        target = place(rest(me + j, peers))
        return pltpu.make_async_remote_copy(
            src_ref=parts_ref.at[
                target["sky"], pl.ds(pl.multiple_of(target["sub"] * rows, rows), rows)
            ],
            dst_ref=arrived.at[me],
            send_sem=part_send.at[j],
            recv_sem=part_recv.at[j],
            device_id=target,
            device_id_type=MESH,
        )

    def expect(j):
        source = rest(me + peers - j, peers)
        return pltpu.make_async_remote_copy(
            src_ref=parts_ref.at[0, pl.ds(0, rows)],
            dst_ref=arrived.at[source],
            send_sem=part_send.at[j],
            recv_sem=part_recv.at[j],
            device_id=place(source),
            device_id_type=MESH,
        )

    def half(j):
        target = rest(sub + j, sub_count)
        return pltpu.make_async_remote_copy(
            src_ref=basis_ref.at[:, pl.ds(pl.multiple_of(target * degrees, degrees), degrees)],
            dst_ref=halves.at[sub],
            send_sem=half_send.at[j],
            recv_sem=half_recv.at[j],
            device_id={"sub": target},
            device_id_type=MESH,
        )

    def expect_half(j):
        source = rest(sub + sub_count - j, sub_count)
        return pltpu.make_async_remote_copy(
            src_ref=basis_ref.at[:, pl.ds(0, degrees)],
            dst_ref=halves.at[source],
            send_sem=half_send.at[j],
            recv_sem=half_recv.at[j],
            device_id={"sub": source},
            device_id_type=MESH,
        )

    own = pltpu.make_async_copy(
        basis_ref.at[:, pl.ds(pl.multiple_of(sub * degrees, degrees), degrees)],
        halves.at[sub],
        own_sem,
    )
    own.start()

    def fetch_particles():
        for fetch in fetches[:-6]:
            fetch.wait()

    def fetch_tables():
        for fetch in fetches[-6:]:
            fetch.wait()

    def early():
        pl.semaphore_wait(barrier, peers - 1)
        for j in range(1, sub_count):
            half(j).start()

    deposit(
        sky_count, blocks, cycle_ref, pixel_ref, mass_ref, block_ref, shell_ref, place_ref,
        spectrum_ref, turns_ref, parts_ref, key_ref, fine_ref, high_ref, low_ref, hist_ref,
        fetch_particles, fetch_tables, early,
    )

    @pl.loop(1, peers, unroll=peers <= 16)
    def _(j):
        send(j).start()

    arrived[me] = parts_ref[sky, pl.ds(pl.multiple_of(sub * rows, rows), rows)]

    @pl.loop(1, peers, unroll=peers <= 16)
    def _(j):
        expect(j).wait_recv()

    group = sky_count * sub_count
    sums = [jnp.sum(arrived[x * group : (x + 1) * group], axis=0) for x in range(shell_count)]
    modes = jnp.concatenate(sums, axis=0) * (2.0 * math.pi / NP)
    rounded[sub] = modes.astype(jnp.bfloat16)

    def hand(j):
        return pltpu.make_async_remote_copy(
            src_ref=rounded.at[sub],
            dst_ref=rounded.at[sub],
            send_sem=sum_send.at[j],
            recv_sem=sum_recv.at[j],
            device_id={"sub": rest(sub + j, sub_count)},
            device_id_type=MESH,
        )

    def expect_sum(j):
        source = rest(sub + sub_count - j, sub_count)
        return pltpu.make_async_remote_copy(
            src_ref=rounded.at[sub],
            dst_ref=rounded.at[source],
            send_sem=sum_send.at[j],
            recv_sem=sum_recv.at[j],
            device_id={"sub": source},
            device_id_type=MESH,
        )

    for j in range(1, sub_count):
        hand(j).start()
    for j in range(1, sub_count):
        expect_sum(j).wait_recv()
    summed = [rounded[c].astype(jnp.float32) for c in range(sub_count)]
    folded = [None] * per
    for x in range(shell_count):
        modes = jnp.concatenate([kept[x * rows : (x + 1) * rows] for kept in summed], axis=0)
        for s in range(SHELL_DEV):
            part = modes[s * blocks : (s + 1) * blocks]
            lens = x * SHELL_DEV + s
            for i in range(per):
                source = shell * per + i
                weight = jnp.where(lens <= source, weight_ref[source, lens], 0.0)
                term = weight * part
                folded[i] = term if folded[i] is None else folded[i] + term
    folded = jnp.concatenate(split(jnp.concatenate(folded, axis=0)), axis=0)
    width = folded.shape[1]
    to = lax.broadcasted_iota(jnp.int32, (width, width), 0)
    within = rest(to, 2 * orders)
    source = to - within + rest(to, 2) * orders + quotient(within, 2)
    swap = source == lax.broadcasted_iota(jnp.int32, (width, width), 1)
    swap = jnp.where(swap, 1.0, 0.0).astype(jnp.bfloat16)
    coefficients = dot(swap, folded, 1).astype(jnp.bfloat16)
    depth = orders * cycles
    span = 2 * orders
    lane = lax.broadcasted_iota(jnp.int32, (2 * per * blocks, depth), 1)
    row = lax.broadcasted_iota(jnp.int32, (2 * per * blocks, depth), 0)
    lane_out = lax.broadcasted_iota(jnp.int32, (span, depth), 1)
    diagonal = quotient(lane_out, cycles) == quotient(
        lax.broadcasted_iota(jnp.int32, (span, depth), 0), 2
    )
    even = rest(lane_out, CYCLE_DEV) == 0
    turn = quotient(rest(lane, cycles), CYCLE_DEV)
    left = []
    for h in range(sub_count):
        strips = []
        for piece in range(2):
            for i in range(per):
                block = (piece * per + i) * blocks + h * (cycles // CYCLE_DEV) + turn
                pick = jnp.where(row == block, 1.0, 0.0).astype(jnp.bfloat16)
                spread = dot(coefficients, pick)
                chosen = jnp.where(even, spread[:span], spread[span:])
                strips.append(jnp.where(diagonal, chosen, 0.0).astype(jnp.bfloat16))
        left.append(jnp.concatenate(strips, axis=0))
    own.wait()
    for j in range(1, sub_count):
        expect_half(j).wait_recv()
    step = 512
    for first in range(0, degrees, step):
        columns = slice(first, first + step)
        result = None
        for h in range(sub_count):
            term = jnp.dot(left[h], halves[h, :, columns], preferred_element_type=jnp.float32)
            result = term if result is None else result + term
        result = result[: per * span] + result[per * span :]
        for i in range(per):
            out_ref[i, :, :, columns] = result[i * span : (i + 1) * span].reshape(orders, 2, step)
    for j in range(1, sub_count):
        half(j).wait_send()
        hand(j).wait_send()

    @pl.loop(1, peers, unroll=peers <= 16)
    def _(j):
        send(j).wait_send()


def body(
    part_cycle,
    part_pixel,
    part_mass,
    tile_block,
    tile_shell,
    tile_pixel,
    harmonic_basis,
    lens_weight,
):
    shell_count, sky_count, sub_count = (
        lax.axis_size("shell"),
        lax.axis_size("sky"),
        lax.axis_size("sub"),
    )
    owners = sky_count * sub_count
    peers = shell_count * owners
    tiles, particles = part_cycle.shape[1:]
    orders, cycles, degrees = harmonic_basis.shape
    per = lens_weight.shape[0] // shell_count
    share = degrees // sub_count
    bins = SHELL_DEV * owners
    width = 2 * CYCLE_DEV * orders
    spectrum, turns = tables()
    result = pl.pallas_call(
        functools.partial(kernel, (shell_count, sky_count, sub_count), per, owners, cycles),
        out_shape=pltpu.VMEM((per, orders, 2, share), jnp.float32),
        in_specs=[pl.BlockSpec(memory_space=pltpu.HBM)] * 10,
        out_specs=pl.BlockSpec(memory_space=pltpu.VMEM),
        scratch_shapes=[
            pltpu.VMEM((particles // SIDE, tiles, SIDE), jnp.int32),
            pltpu.VMEM((particles // SIDE, tiles, SIDE), jnp.int32),
            pltpu.VMEM((particles // SIDE, tiles, SIDE), jnp.float32),
            pltpu.VMEM((1, tiles), jnp.int32),
            pltpu.VMEM((1, tiles), jnp.int32),
            pltpu.VMEM((1, tiles), jnp.int32),
            pltpu.VMEM(spectrum.shape, jnp.float32),
            pltpu.VMEM(turns.shape, jnp.float32),
            pltpu.SMEM(lens_weight.shape, jnp.float32),
            pltpu.VMEM((particles // SIDE, tiles, SIDE), jnp.int32),
            pltpu.VMEM((particles // SIDE, tiles, SIDE), jnp.float32),
            pltpu.VMEM((particles // SIDE, tiles, SIDE), jnp.float32),
            pltpu.VMEM((particles // SIDE, tiles, SIDE), jnp.float32),
            pltpu.VMEM((2, tiles * CYCLE_DEV * TP // (2 * SIDE), SIDE), jnp.float32),
            pltpu.VMEM((sky_count, bins, width), jnp.float32),
            pltpu.VMEM((sub_count, orders * cycles, share), jnp.bfloat16),
            pltpu.VMEM((peers, bins // sub_count, width), jnp.float32),
            pltpu.VMEM((sub_count, shell_count * bins // sub_count, width), jnp.bfloat16),
            pltpu.SemaphoreType.DMA((3 * (particles // SIDE) + 6,)),
            pltpu.SemaphoreType.DMA,
            pltpu.SemaphoreType.DMA((sub_count,)),
            pltpu.SemaphoreType.DMA((sub_count,)),
            pltpu.SemaphoreType.DMA((peers,)),
            pltpu.SemaphoreType.DMA((peers,)),
            pltpu.SemaphoreType.DMA((sub_count,)),
            pltpu.SemaphoreType.DMA((sub_count,)),
        ],
        compiler_params=pltpu.CompilerParams(
            collective_id=0, has_side_effects=True, vmem_limit_bytes=60 << 20
        ),
        name="modes",
    )(
        part_cycle[0],
        part_pixel[0],
        part_mass[0],
        tile_block.reshape(1, tiles),
        tile_shell,
        tile_pixel,
        spectrum,
        turns,
        lens_weight,
        harmonic_basis.reshape(orders * cycles, degrees),
    )
    return result


def solution(mesh):
    return jax.shard_map(
        body,
        mesh=mesh,
        in_specs=(
            P("shell", ("sky", "sub"), None),
            P("shell", ("sky", "sub"), None),
            P("shell", ("sky", "sub"), None),
            P("shell", ("sky", "sub"), None),
            P("shell", ("sky", "sub")),
            P("shell", ("sky", "sub")),
            P("sky", "sub", None),
            P(),
        ),
        out_specs=P(("groups", "shell"), "sky", None, "sub"),
        check_vma=False,
    )
```

```python
import functools
import math

import jax
import jax.numpy as jnp
import numpy as np
from jax import lax
from jax.experimental import pallas as pl
from jax.experimental.pallas import tpu as pltpu
from jax.sharding import PartitionSpec as P

NP = 8192
M = 128
TP = 128
CYCLE_DEV = 2
SHELL_DEV = 2
NBLK = NP // TP

MESH = pl.DeviceIdType.MESH


def tables():
    pixel = np.arange(TP, dtype=np.float64)
    smooth = np.exp(-((pixel[:, None] - pixel[None, :]) ** 2) / 18.0)
    orders = np.arange(M)
    angle = 2.0 * math.pi * ((np.arange(TP)[:, None] * orders[None, :]) % NP) / NP
    turn = 2.0 * math.pi * ((np.arange(NBLK)[:, None] * TP * orders[None, :]) % NP) / NP
    spectrum = np.concatenate([smooth @ np.cos(angle), -(smooth @ np.sin(angle))], axis=1)
    turns = np.concatenate([np.cos(turn), -np.sin(turn)], axis=1)

    def split(table):
        high = table.astype(jnp.bfloat16)
        low = (table - high.astype(np.float64)).astype(jnp.bfloat16)
        return np.concatenate([high, low], axis=0).astype(np.float32)

    return split(spectrum), split(turns)


def split(values):
    high = values.astype(jnp.bfloat16)
    return high, (values - high.astype(jnp.float32)).astype(jnp.bfloat16)


def dot(one, two, right=0):
    return lax.dot_general(
        one, two, (((1,), (right,)), ((), ())), preferred_element_type=jnp.float32
    )


FINE = 32
SIDE = 128


def quotient(value, by):
    return value >> (by.bit_length() - 1) if by & (by - 1) == 0 else value // by


def rest(value, by):
    return value & (by - 1) if by & (by - 1) == 0 else value % by


def deposit(
    sky_count, owners, cycle_ref, pixel_ref, mass_ref, block_ref, shell_ref, place_ref, spectrum_ref,
    turns_ref, out_ref, key_ref, fine_ref, high_ref, low_ref, hist_ref, fetch_particles, fetch_tables,
    early,
):
    halves, tiles = pixel_ref.shape[:2]
    coarse = TP // FINE
    bundle = 2 * SIDE // FINE
    groups = tiles // bundle
    keys = CYCLE_DEV * coarse
    fetch_particles()
    masses = mass_ref[...]
    pixels = pixel_ref[...]
    high = masses.astype(jnp.bfloat16).astype(jnp.float32)
    high_ref[...] = high
    low_ref[...] = masses - high
    fine_ref[...] = rest(pixels, FINE).astype(jnp.float32)
    key_ref[...] = cycle_ref[...] * coarse + quotient(pixels, FINE)
    fine_ids = lax.broadcasted_iota(jnp.int32, (FINE, SIDE), 0)
    fine_ids = fine_ids.astype(jnp.float32).astype(jnp.bfloat16)
    ones, zeros = jnp.ones((FINE, SIDE), jnp.bfloat16), jnp.zeros((FINE, SIDE), jnp.bfloat16)
    key_ids = lax.broadcasted_iota(jnp.int32, (keys, SIDE), 0)
    same = (
        quotient(lax.broadcasted_iota(jnp.int32, (bundle * keys, bundle * FINE), 0), keys)
        == quotient(lax.broadcasted_iota(jnp.int32, (bundle * keys, bundle * FINE), 1), FINE)
    )

    def group(g, carry):
        spread, highs, lows = [], [], []
        for t in range(bundle):
            row = pl.ds(t * groups + g, 1)
            spread_t, high_t, low_t = [], [], []
            for h in range(halves):
                fine = jnp.broadcast_to(fine_ref[h, row, :], (FINE, SIDE)).astype(jnp.bfloat16)
                spread_t.append(jnp.where(fine == fine_ids, ones, zeros))
                here = jnp.broadcast_to(key_ref[h, row, :], (keys, SIDE)) == key_ids
                high_t.append(
                    jnp.where(here, jnp.broadcast_to(high_ref[h, row, :], (keys, SIDE)), 0.0)
                )
                low_t.append(
                    jnp.where(here, jnp.broadcast_to(low_ref[h, row, :], (keys, SIDE)), 0.0)
                )
            spread.append(jnp.concatenate(spread_t, axis=1))
            highs.append(jnp.concatenate(high_t, axis=1))
            lows.append(jnp.concatenate(low_t, axis=1))
        weights = jnp.concatenate(highs + lows, axis=0).astype(jnp.bfloat16)
        pairs = dot(weights, jnp.concatenate(spread, axis=0), 1)
        count = bundle * keys
        pairs = jnp.where(same, pairs[:count] + pairs[count:], 0.0)
        own = jnp.sum(pairs.reshape(bundle, keys, bundle * FINE), axis=0)
        at = pl.ds(pl.multiple_of(g * keys, keys), keys)
        for side in range(bundle * FINE // SIDE):
            hist_ref[side, at, :] = own[:, side * SIDE : (side + 1) * SIDE]
        return carry

    lax.fori_loop(0, groups, group, 0, unroll=32)
    early()
    fetch_tables()
    lane = quotient(lax.broadcasted_iota(jnp.int32, (groups, SIDE), 1), FINE)
    strips = [
        [hist_ref[side, pl.ds(key, groups, stride=keys), :] for key in range(keys)]
        for side in range(bundle * FINE // SIDE)
    ]
    hist = []
    for c in range(CYCLE_DEV):
        for t in range(bundle):
            side, offset = t * FINE // SIDE, t * FINE % SIDE
            joined = None
            for x in range(coarse):
                shift = (x * FINE - offset) % SIDE
                strip = strips[side][c * coarse + x]
                moved = strip if shift == 0 else pltpu.roll(strip, shift, 1)
                joined = moved if joined is None else jnp.where(lane == x, moved, joined)
            hist.append(joined)
    high, low = split(jnp.concatenate(hist, axis=0))
    spectrum = spectrum_ref[...].astype(jnp.bfloat16)
    modes = dot(high, spectrum[:TP]) + dot(low, spectrum[:TP]) + dot(high, spectrum[TP:])
    position = rest(lax.broadcasted_iota(jnp.int32, (2 * NBLK, tiles), 0), NBLK) == place_ref[...]
    position = jnp.where(position, 1.0, 0.0).T.astype(jnp.bfloat16)
    turns = dot(position, turns_ref[...].astype(jnp.bfloat16))
    cosine, sine = turns[:, :M], turns[:, M:]
    turned = []
    for c in range(CYCLE_DEV):
        real = modes[c * tiles : (c + 1) * tiles, :M]
        imag = modes[c * tiles : (c + 1) * tiles, M:]
        turned += [real * cosine - imag * sine, real * sine + imag * cosine]
    bins = SHELL_DEV * owners
    key = shell_ref[...] * owners + block_ref[...]
    hot = lax.broadcasted_iota(jnp.int32, (bins, tiles), 0) == key
    hot = jnp.where(hot, 1.0, 0.0).astype(jnp.bfloat16)
    high, low = split(jnp.concatenate(turned, axis=1))
    binned = dot(hot, high) + dot(hot, low)
    pieces = [binned[:, n * M : (n + 1) * M] for n in range(2 * CYCLE_DEV)]
    near = math.exp(-0.5)
    pieces = [
        pieces[2 * k + part] + near * pieces[2 * (1 - k) + part]
        for k in range(CYCLE_DEV)
        for part in range(2)
    ]
    share = M // sky_count
    width = len(pieces) * share
    lane = quotient(lax.broadcasted_iota(jnp.int32, (bins, M), 1), share)
    for z in range(sky_count):
        message = None
        for n, piece in enumerate(pieces):
            shift = (n - z) * share % M
            moved = piece if shift == 0 else pltpu.roll(piece, shift, 1)
            message = moved if message is None else jnp.where(lane == n, moved, message)
        out_ref[z] = message[:, :width]


def kernel(
    counts, per, blocks, cycles, cycle_hbm, pixel_hbm, mass_hbm, block_hbm, shell_hbm, place_hbm,
    spectrum_hbm, turns_hbm, weight_hbm, basis_ref, out_ref,
    cycle_ref, pixel_ref, mass_ref, block_ref, shell_ref, place_ref, spectrum_ref, turns_ref,
    weight_ref, key_ref, fine_ref, high_ref, low_ref, hist_ref, parts_ref,
    halves, arrived, fetch_sem, own_sem, half_send, half_recv, part_send, part_recv,
):
    fetches = [
        pltpu.make_async_copy(source, target, fetch_sem.at[n])
        for n, (source, target) in enumerate(
            (
                *(
                    (array.at[:, h * SIDE : (h + 1) * SIDE], held.at[h])
                    for array, held in (
                        (cycle_hbm, cycle_ref),
                        (pixel_hbm, pixel_ref),
                        (mass_hbm, mass_ref),
                    )
                    for h in range(cycle_ref.shape[0])
                ),
                (spectrum_hbm, spectrum_ref),
                (turns_hbm, turns_ref),
                (block_hbm, block_ref),
                (shell_hbm, shell_ref),
                (place_hbm, place_ref),
                (weight_hbm, weight_ref),
            )
        )
    ]
    for fetch in fetches:
        fetch.start()
    shell_count, sky_count, sub_count = counts
    shell, sky, sub = lax.axis_index("shell"), lax.axis_index("sky"), lax.axis_index("sub")
    peers = shell_count * sky_count * sub_count
    me = (shell * sky_count + sky) * sub_count + sub
    degrees = halves.shape[2]
    orders = basis_ref.shape[0] // cycles

    def place(rank):
        return dict(
            shell=quotient(rank, sky_count * sub_count),
            sky=rest(quotient(rank, sub_count), sky_count),
            sub=rest(rank, sub_count),
        )

    barrier = pltpu.get_barrier_semaphore()

    @pl.loop(1, peers, unroll=peers <= 16)
    def _(j):
        pl.semaphore_signal(
            barrier, inc=1, device_id=place(rest(me + j, peers)), device_id_type=MESH
        )

    def send(j):
        target = place(rest(me + j, peers))
        return pltpu.make_async_remote_copy(
            src_ref=parts_ref.at[target["sky"]],
            dst_ref=arrived.at[me],
            send_sem=part_send.at[j],
            recv_sem=part_recv.at[j],
            device_id=target,
            device_id_type=MESH,
        )

    def expect(j):
        source = rest(me + peers - j, peers)
        return pltpu.make_async_remote_copy(
            src_ref=parts_ref.at[0],
            dst_ref=arrived.at[source],
            send_sem=part_send.at[j],
            recv_sem=part_recv.at[j],
            device_id=place(source),
            device_id_type=MESH,
        )

    def half(j):
        target = rest(sub + j, sub_count)
        return pltpu.make_async_remote_copy(
            src_ref=basis_ref.at[:, pl.ds(pl.multiple_of(target * degrees, degrees), degrees)],
            dst_ref=halves.at[sub],
            send_sem=half_send.at[j],
            recv_sem=half_recv.at[j],
            device_id={"sub": target},
            device_id_type=MESH,
        )

    def expect_half(j):
        source = rest(sub + sub_count - j, sub_count)
        return pltpu.make_async_remote_copy(
            src_ref=basis_ref.at[:, pl.ds(0, degrees)],
            dst_ref=halves.at[source],
            send_sem=half_send.at[j],
            recv_sem=half_recv.at[j],
            device_id={"sub": source},
            device_id_type=MESH,
        )

    own = pltpu.make_async_copy(
        basis_ref.at[:, pl.ds(pl.multiple_of(sub * degrees, degrees), degrees)],
        halves.at[sub],
        own_sem,
    )
    own.start()

    def fetch_particles():
        for fetch in fetches[:-6]:
            fetch.wait()

    def fetch_tables():
        for fetch in fetches[-6:]:
            fetch.wait()

    def early():
        pl.semaphore_wait(barrier, peers - 1)
        for j in range(1, sub_count):
            half(j).start()

    deposit(
        sky_count, blocks, cycle_ref, pixel_ref, mass_ref, block_ref, shell_ref, place_ref,
        spectrum_ref, turns_ref, parts_ref, key_ref, fine_ref, high_ref, low_ref, hist_ref,
        fetch_particles, fetch_tables, early,
    )

    @pl.loop(1, peers, unroll=peers <= 16)
    def _(j):
        send(j).start()

    width = parts_ref.shape[2]
    to = lax.broadcasted_iota(jnp.int32, (width, width), 0)
    within = rest(to, 2 * orders)
    source = to - within + rest(to, 2) * orders + quotient(within, 2)
    swap = source == lax.broadcasted_iota(jnp.int32, (width, width), 1)
    swap = jnp.where(swap, 1.0, 0.0).astype(jnp.bfloat16)
    depth = orders * cycles
    span = 2 * orders
    lane = lax.broadcasted_iota(jnp.int32, (2 * per * blocks, depth), 1)
    row = lax.broadcasted_iota(jnp.int32, (2 * per * blocks, depth), 0)
    lane_out = lax.broadcasted_iota(jnp.int32, (span, depth), 1)
    diagonal = quotient(lane_out, cycles) == quotient(
        lax.broadcasted_iota(jnp.int32, (span, depth), 0), 2
    )
    even = rest(lane_out, CYCLE_DEV) == 0
    turn = quotient(rest(lane, cycles), CYCLE_DEV)
    picks = []
    for h in range(sub_count):
        for place_of in range(2 * per):
            block = place_of * blocks + h * (cycles // CYCLE_DEV) + turn
            picks.append(jnp.where(row == block, 1.0, 0.0).astype(jnp.bfloat16))
    arrived[me] = parts_ref[sky]

    @pl.loop(1, peers, unroll=peers <= 16)
    def _(j):
        expect(j).wait_recv()

    group = sky_count * sub_count
    folded = [None] * per
    for x in range(shell_count):
        total = jnp.sum(arrived[x * group : (x + 1) * group], axis=0)
        modes = (total * (2.0 * math.pi / NP)).astype(jnp.bfloat16).astype(jnp.float32)
        for s in range(SHELL_DEV):
            part = modes[s * blocks : (s + 1) * blocks]
            lens = x * SHELL_DEV + s
            for i in range(per):
                source = shell * per + i
                weight = jnp.where(lens <= source, weight_ref[source, lens], 0.0)
                term = weight * part
                folded[i] = term if folded[i] is None else folded[i] + term
    folded = jnp.concatenate(split(jnp.concatenate(folded, axis=0)), axis=0)
    coefficients = dot(swap, folded, 1).astype(jnp.bfloat16)
    left = []
    for h in range(sub_count):
        rows = []
        for piece in range(2):
            for i in range(per):
                spread = dot(coefficients, picks[(h * 2 + piece) * per + i])
                chosen = jnp.where(even, spread[:span], spread[span:])
                rows.append(jnp.where(diagonal, chosen, 0.0).astype(jnp.bfloat16))
        left.append(jnp.concatenate(rows, axis=0))
    own.wait()
    for j in range(1, sub_count):
        expect_half(j).wait_recv()
    step = 512
    for first in range(0, degrees, step):
        columns = slice(first, first + step)
        result = None
        for h in range(sub_count):
            term = jnp.dot(left[h], halves[h, :, columns], preferred_element_type=jnp.float32)
            result = term if result is None else result + term
        result = result[: per * span] + result[per * span :]
        for i in range(per):
            out_ref[i, :, :, columns] = result[i * span : (i + 1) * span].reshape(orders, 2, step)
    for j in range(1, sub_count):
        half(j).wait_send()

    @pl.loop(1, peers, unroll=peers <= 16)
    def _(j):
        send(j).wait_send()


def body(
    part_cycle,
    part_pixel,
    part_mass,
    tile_block,
    tile_shell,
    tile_pixel,
    harmonic_basis,
    lens_weight,
):
    shell_count, sky_count, sub_count = (
        lax.axis_size("shell"),
        lax.axis_size("sky"),
        lax.axis_size("sub"),
    )
    owners = sky_count * sub_count
    peers = shell_count * owners
    tiles, particles = part_cycle.shape[1:]
    orders, cycles, degrees = harmonic_basis.shape
    per = lens_weight.shape[0] // shell_count
    share = degrees // sub_count
    bins = SHELL_DEV * owners
    width = 2 * CYCLE_DEV * orders
    spectrum, turns = tables()
    result = pl.pallas_call(
        functools.partial(kernel, (shell_count, sky_count, sub_count), per, owners, cycles),
        out_shape=pltpu.VMEM((per, orders, 2, share), jnp.float32),
        in_specs=[pl.BlockSpec(memory_space=pltpu.HBM)] * 10,
        out_specs=pl.BlockSpec(memory_space=pltpu.VMEM),
        scratch_shapes=[
            pltpu.VMEM((particles // SIDE, tiles, SIDE), jnp.int32),
            pltpu.VMEM((particles // SIDE, tiles, SIDE), jnp.int32),
            pltpu.VMEM((particles // SIDE, tiles, SIDE), jnp.float32),
            pltpu.VMEM((1, tiles), jnp.int32),
            pltpu.VMEM((1, tiles), jnp.int32),
            pltpu.VMEM((1, tiles), jnp.int32),
            pltpu.VMEM(spectrum.shape, jnp.float32),
            pltpu.VMEM(turns.shape, jnp.float32),
            pltpu.SMEM(lens_weight.shape, jnp.float32),
            pltpu.VMEM((particles // SIDE, tiles, SIDE), jnp.int32),
            pltpu.VMEM((particles // SIDE, tiles, SIDE), jnp.float32),
            pltpu.VMEM((particles // SIDE, tiles, SIDE), jnp.float32),
            pltpu.VMEM((particles // SIDE, tiles, SIDE), jnp.float32),
            pltpu.VMEM((2, tiles * CYCLE_DEV * TP // (2 * SIDE), SIDE), jnp.float32),
            pltpu.VMEM((sky_count, bins, width), jnp.float32),
            pltpu.VMEM((sub_count, orders * cycles, share), jnp.bfloat16),
            pltpu.VMEM((peers, bins, width), jnp.float32),
            pltpu.SemaphoreType.DMA((3 * (particles // SIDE) + 6,)),
            pltpu.SemaphoreType.DMA,
            pltpu.SemaphoreType.DMA((sub_count,)),
            pltpu.SemaphoreType.DMA((sub_count,)),
            pltpu.SemaphoreType.DMA((peers,)),
            pltpu.SemaphoreType.DMA((peers,)),
        ],
        compiler_params=pltpu.CompilerParams(
            collective_id=0, has_side_effects=True, vmem_limit_bytes=60 << 20
        ),
        name="modes",
    )(
        part_cycle[0],
        part_pixel[0],
        part_mass[0],
        tile_block.reshape(1, tiles),
        tile_shell,
        tile_pixel,
        spectrum,
        turns,
        lens_weight,
        harmonic_basis.reshape(orders * cycles, degrees),
    )
    return result


def solution(mesh):
    return jax.shard_map(
        body,
        mesh=mesh,
        in_specs=(
            P("shell", ("sky", "sub"), None),
            P("shell", ("sky", "sub"), None),
            P("shell", ("sky", "sub"), None),
            P("shell", ("sky", "sub"), None),
            P("shell", ("sky", "sub")),
            P("shell", ("sky", "sub")),
            P("sky", "sub", None),
            P(),
        ),
        out_specs=P(("groups", "shell"), "sky", None, "sub"),
        check_vma=False,
    )
```
